128 devices in a mesh: row: 16 (over x, z), col: 8 (over y, core).
Axes of the slice: x: 4, y: 4, z: 4, core: 2. Of those that a mesh axis runs over, the one named last changes fastest.
Arguments:
- hamiltonian: float32 [18432, 18432], P('row', 'col'), may hold values from -6 to 6, as said below
- panel: float32 [18432, 128], P(('row', 'col')), may hold values from -0.03125 to 0.03125
Outputs:
- updated: float32 [18432, 18432], P('row', 'col')
The draws below stay inside these ranges and needn't reach their ends.
Inputs may be any that keep to these rules, and one draw needn't show every extreme that they name: `hamiltonian`: H is symmetric: the entry at stored row p and stored column q equals the entry whose stored row and column stand for the two global indices swapped.
All inputs are finite; a program needn't handle non-finite values.
Results may differ from the reference program's by a relative error of at most 0.0002.
Values sent between devices are 32-bit elements; how exact they have to be, the bound alone decides.
A program may use at most 128 MiB of HBM per device.

```python
import jax
import jax.numpy as jnp
from jax import lax

B = 128
N = 18432
N_ROW = 16
N_COL = 8


def stored_positions(count, groups, block_width):
    position = jnp.arange(count, dtype=jnp.int32)
    per_group = count // groups
    group_index = position // per_group
    inside = position % per_group
    return (inside // block_width * groups + group_index) * block_width + inside % block_width


def draw_hamiltonian(key, part):
    sampled = jax.random.truncated_normal(key, -4.0, 4.0, (N, N), jnp.float32)
    symmetric = (sampled + sampled.T) * 0.5 ** 0.5
    row_order = stored_positions(N, N_ROW, B)
    col_order = stored_positions(N, N_COL, B)
    return jnp.take(jnp.take(symmetric, row_order, axis=0), col_order, axis=1)


def shard_levels(key, extent, split, smallest, top_value):
    def one(axis_at, blocks):
        draws = jax.random.uniform(jax.random.fold_in(jax.random.fold_in(key, 6), axis_at), (blocks,), jnp.float32, smallest / len(split), top_value / len(split))
        return jnp.repeat(jnp.exp(draws), extent[axis_at] // blocks).reshape((-1,) + (1,) * (len(extent) - axis_at - 1))

    loudness = one(*split[0])
    for cut in split[1:]:
        loudness = loudness * one(*cut)
    return loudness


def centred(stream_key, extent, spread, reach, cuts=(), held_as=jnp.bfloat16):
    gain = shard_levels(stream_key, extent, cuts, -0.22, 0.18) if cuts else 1.0
    values = jax.random.normal(stream_key, extent, jnp.float32) * spread * gain
    return jnp.minimum(jnp.maximum(values, -reach), reach).astype(held_as)


def setup_inputs(seed: int = 0) -> dict:
    seeds = jax.random.split(jax.random.key(seed), 3)
    hamiltonian = draw_hamiltonian(jax.random.fold_in(seeds[2], 71), 0)
    panel = centred(seeds[1], (N, B), (2 * N) ** -0.5, 0.03125, ((0, 128),), jnp.float32)
    return dict(hamiltonian=hamiltonian, panel=panel)


highest = lax.Precision.HIGHEST


def matmul(left, right):
    return jnp.dot(left, right, precision=highest, preferred_element_type=jnp.float32)


def stored_global(count, groups, block_width):
    position = jnp.arange(count, dtype=jnp.int32)
    per_group = count // groups
    group_index = position // per_group
    inside = position % per_group
    return ((inside // block_width) * groups + group_index) * block_width + inside % block_width


def shape_panel(panel_raw, global_rows, block_width):
    global_block = global_rows // block_width
    within = global_rows % block_width
    column_ids = jnp.arange(panel_raw.shape[1], dtype=jnp.int32)
    below = column_ids[None, :] < within[:, None]
    on_diagonal = column_ids[None, :] == within[:, None]
    unit_block = jnp.where(below, panel_raw, jnp.where(on_diagonal, 1.0, 0.0))
    kept = jnp.where((global_block == 1)[:, None], unit_block, 0.0)
    return jnp.where((global_block >= 2)[:, None], panel_raw, kept).astype(jnp.float32)


def upper_inverse(gram_matrix):
    width = gram_matrix.shape[0]
    diagonal_half = jnp.diag(gram_matrix) * 0.5
    nilpotent = jnp.triu(gram_matrix, 1) / diagonal_half[:, None]
    identity_matrix = jnp.eye(width, dtype=gram_matrix.dtype)
    power = -nilpotent
    result = identity_matrix + power
    for level in range(width.bit_length()):
        power = matmul(power, power)
        result = matmul(result, identity_matrix + power)
    return result / diagonal_half[None, :]


def compact_factors(gram_matrix, cross_term):
    block_factor = upper_inverse(gram_matrix)
    middle = matmul(matmul(block_factor.T, cross_term), block_factor)
    return block_factor, middle


def reference(hamiltonian, panel):
    row_map = stored_global(N, N_ROW, B)
    col_map = stored_global(N, N_COL, B)
    v_rows = shape_panel(panel, row_map, B)
    inverse_rows = jnp.zeros((N,), jnp.int32).at[row_map].set(jnp.arange(N, dtype=jnp.int32))
    v_cols = jnp.take(v_rows, inverse_rows[col_map], axis=0)
    p_rows = matmul(hamiltonian, v_cols)
    gram_matrix = matmul(v_rows.T, v_rows)
    cross_term = matmul(v_rows.T, p_rows)
    block_factor, middle = compact_factors(gram_matrix, cross_term)
    y_rows = matmul(p_rows, block_factor) - 0.5 * matmul(v_rows, middle)
    p_cols = lax.dot_general(hamiltonian, v_rows, (((0,), (0,)), ((), ())), precision=highest, preferred_element_type=jnp.float32)
    y_cols = matmul(p_cols, block_factor) - 0.5 * matmul(v_cols, middle)
    left_side = jnp.concatenate([v_rows, y_rows], axis=1)
    right_side = jnp.concatenate([y_cols, v_cols], axis=1)
    updated = hamiltonian - lax.dot_general(left_side, right_side, (((1,), (1,)), ((), ())), precision=highest, preferred_element_type=jnp.float32)
    return updated
```

```python
import jax
import jax.numpy as jnp
from jax import lax
from jax.experimental import pallas as pl
from jax.experimental.pallas import tpu as pltpu
from jax.sharding import PartitionSpec as P

B = 128
R = 16
C = 8
MESH = pl.DeviceIdType.MESH
F32 = jnp.float32
BF16 = jnp.bfloat16
HIGHEST = lax.Precision.HIGHEST
NN = (((1,), (0,)), ((), ()))
NT = (((1,), (1,)), ((), ()))
TN = (((0,), (0,)), ((), ()))


def dot6(a, b, dims=NN):
    return lax.dot_general(a, b, dims, precision=HIGHEST, preferred_element_type=F32)


def dot1(a, b, dims=NN):
    return lax.dot_general(a, b, dims, preferred_element_type=F32)


def halves(v):
    hi = v.astype(BF16)
    return hi, (v - hi.astype(F32)).astype(BF16)


def mod4(v):
    return lax.rem(v + 8, 4)


def panel_kernel(
    h_ref, panel_ref, whi_ref, wlo_ref, zhi_ref, zlo_ref,
    hbuf, hhi, hlo, vw, rows, cols, acc, own, sib_in, ring_in, ring_out,
    part, ar1, ar2, ar3, arout, power, inverse,
    h_sem, ysend, yrecv, psend, precv, sib_send, sib_recv, ring_send, ring_recv, ar_send, ar_recv,
):
    row = lax.axis_index("row")
    col = lax.axis_index("col")
    x, z = row // 4, lax.rem(row, 4)
    y, core = col // 2, lax.rem(col, 2)
    other = col + 1 - 2 * core
    piece = panel_ref.shape[0]
    local_rows = hbuf.shape[0]
    blocks = local_rows // B

    def at_y(off):
        return (row, mod4(y + off) * 2 + core)

    peers = [(row, lax.rem(col + o, C)) for o in range(1, C)]
    x_peers = [(mod4(x + o) * 4 + z, col) for o in range(1, 4)]
    z_peers = [(x * 4 + mod4(z + o), col) for o in range(1, 4)]
    barrier = pltpu.get_barrier_semaphore()
    for peer in peers + x_peers + z_peers:
        pl.semaphore_signal(barrier, inc=1, device_id=peer, device_id_type=MESH)

    n_h = h_sem.shape[0]
    h_rows = local_rows // n_h
    h_copies = [
        pltpu.make_async_copy(
            h_ref.at[pl.ds(i * h_rows, h_rows)], hbuf.at[pl.ds(i * h_rows, h_rows)], h_sem.at[i]
        )
        for i in range(n_h)
    ]
    for copy in h_copies:
        copy.start()

    position = col * piece + lax.broadcasted_iota(jnp.int32, (piece, B), 0)
    column = lax.broadcasted_iota(jnp.int32, (piece, B), 1)
    global_block = (position >> 7) * R + row
    within = position & (B - 1)
    raw = panel_ref[...]
    unit = jnp.where(column < within, raw, jnp.where(column == within, 1.0, 0.0))
    kept = jnp.where(global_block == 1, unit, 0.0)
    v_piece = jnp.where(global_block >= 2, raw, kept)
    rows[0, col] = v_piece
    part[0] = dot6(v_piece, v_piece, TN)

    pl.semaphore_wait(barrier, len(peers) + len(x_peers) + len(z_peers))

    def remote(src, dst, send, recv, peer):
        return pltpu.make_async_remote_copy(
            src_ref=src, dst_ref=dst, send_sem=send, recv_sem=recv, device_id=peer, device_id_type=MESH
        )

    def reduce_step(ph, step):
        def wait_recv(buf, count):
            pltpu.make_async_copy(buf.at[ph, pl.ds(0, count)], buf.at[ph, pl.ds(0, count)], ar_recv.at[ph, step - 1]).wait()

        if step == 0:
            for peer in peers:
                remote(
                    part.at[ph, pl.ds(pl.multiple_of(peer[1] * 16, 16), 16)], ar1.at[ph, col],
                    ar_send.at[ph, 0], ar_recv.at[ph, 0], peer,
                ).start()
            ar1[ph, col] = part[ph, pl.ds(pl.multiple_of(col * 16, 16), 16)]
        elif step == 1:
            wait_recv(ar1, C - 1)
            ar2[ph, x] = sum(ar1[ph, i] for i in range(C))
            for peer in x_peers:
                remote(ar2.at[ph, x], ar2.at[ph, x], ar_send.at[ph, 1], ar_recv.at[ph, 1], peer).start()
        elif step == 2:
            wait_recv(ar2, 3)
            ar3[ph, z] = sum(ar2[ph, i] for i in range(4))
            for peer in z_peers:
                remote(ar3.at[ph, z], ar3.at[ph, z], ar_send.at[ph, 2], ar_recv.at[ph, 2], peer).start()
        elif step == 3:
            wait_recv(ar3, 3)
            mine = pl.ds(pl.multiple_of(col * 16, 16), 16)
            arout[ph, mine] = sum(ar3[ph, i] for i in range(4))
            for peer in peers:
                remote(arout.at[ph, mine], arout.at[ph, mine], ar_send.at[ph, 3], ar_recv.at[ph, 3], peer).start()
        else:
            pltpu.make_async_copy(
                arout.at[ph, pl.ds(0, 16 * (C - 1))], arout.at[ph, pl.ds(0, 16 * (C - 1))], ar_recv.at[ph, 3]
            ).wait()

    def reduce_finish(ph):
        for step, (buf, count) in enumerate([(ar1, C - 1), (ar2, 3), (ar3, 3), (ar1, C - 1)]):
            pltpu.make_async_copy(buf.at[ph, pl.ds(0, count)], buf.at[ph, pl.ds(0, count)], ar_send.at[ph, step]).wait()

    sign = 1 - 2 * core
    z0 = 2 * lax.rem(y, 2) + core
    dz = mod4((z - z0) * sign)
    dxs = [mod4(x - y // 2 - 2 * s) for s in range(2)]
    depth_z = jnp.minimum(dz, 4 - dz)
    depths = [jnp.minimum(dx, 4 - dx) + depth_z for dx in dxs]
    plane = [
        (mod4(x + 1) * 4 + z, col),
        (mod4(x - 1) * 4 + z, col),
        (x * 4 + mod4(z + sign), col),
        (x * 4 + mod4(z - sign), col),
    ]

    def natural(kk):
        off = (0, -1, 1, 2)[kk // 2]
        return mod4(y + off) * 2 + (core if kk % 2 == 0 else 1 - core)

    def children(i, s):
        turn = (i // 2) % 2
        dx = dxs[s]
        hop = (dx == 1) if turn == 0 else (dx == 3)
        if i % 2 == 0:
            lead = (dz == 0) & (dx == 0)
            line = (dz == 0) & hop
            plus = (lead | line) if turn == 0 else lead
            minus = lead if turn == 0 else (lead | line)
            return [plus, minus, dz == 0, (dz == 0) | (dz == 3)]
        lead = dx == 0
        return [
            (lead | hop) if turn == 0 else lead,
            lead if turn == 0 else (lead | hop),
            (dx == 0) & (dz == 0),
            (dx == 0) & ((dz == 0) | (dz == 3)),
        ]

    def forwards(i, s):
        turn = (i // 2) % 2
        if i % 2 == 0:
            return (dz == 0) | (dz == 3)
        return (dxs[s] == 0) | (dxs[s] == (1 if turn == 0 else 3))

    def plane_send(ph, i, s, source):
        k = natural(i)
        for d, flag in enumerate(children(i, s)):
            @pl.when(flag)
            def _():
                remote(
                    source, cols.at[ph, s, k], psend.at[ph, i % 4, s, d], precv.at[ph, s, k], plane[d]
                ).start()

    def piece_wait(ref, sem):
        pltpu.make_async_copy(ref, ref, sem).wait()

    def line_step(ph, kk):
        k = natural(kk)
        here = rows.at[ph, k]
        if kk > 0:
            piece_wait(here, yrecv.at[ph, k])

        def send(n, peer):
            remote(here, here, ysend.at[ph, n], yrecv.at[ph, k], peer).start()

        if kk == 0:
            send(4, at_y(1))
            send(5, at_y(-1))
        if kk == 2:
            @pl.when(core == 0)
            def _():
                send(6, at_y(1))
        if kk == 4:
            @pl.when(core == 1)
            def _():
                send(6, at_y(-1))
        if kk % 2 == 0:
            send(kk // 2, (row, other))
        for s in range(2):
            @pl.when((dxs[s] == 0) & (dz == 0))
            def _():
                plane_send(ph, kk, s, here)

    def plane_step(ph, i, level):
        for s in range(2):
            @pl.when(forwards(i, s) & (depths[s] == level))
            def _():
                k = natural(i)
                piece_wait(cols.at[ph, s, k], precv.at[ph, s, k])
                plane_send(ph, i, s, cols.at[ph, s, k])

    def gather(ph, extra):
        for tick in range(13):
            if tick < 8:
                line_step(ph, tick)
            for level, skew in ((1, 1), (2, 2), (3, 4)):
                if 0 <= tick - skew < 8:
                    plane_step(ph, tick - skew, level)
            extra(tick)
        for s in range(2):
            for i in range(8):
                k = natural(i)
                root = (dxs[s] == 0) & (dz == 0)
                @pl.when(jnp.logical_not(forwards(i, s)))
                def _():
                    piece_wait(cols.at[ph, s, k], precv.at[ph, s, k])
            @pl.when((dxs[s] == 0) & (dz == 0))
            def _():
                cols[ph, s] = rows[ph]

    def gather_finish(ph):
        for n in range(7):
            piece_wait(rows.at[ph, 0], ysend.at[ph, n])
        for i in range(4):
            for s in range(2):
                for d, flag in enumerate(children(i, s)):
                    @pl.when(flag)
                    def _():
                        two = cols.at[ph, s, pl.ds(0, 2)]
                        piece_wait(two, psend.at[ph, i, s, d])

    def split_h(i):
        h_copies[i].wait()
        hi, lo = halves(hbuf[pl.ds(i * h_rows, h_rows)])
        hhi[pl.ds(i * h_rows, h_rows)] = hi
        hlo[pl.ds(i * h_rows, h_rows)] = lo

    def first_extra(tick):
        if tick == 0:
            reduce_step(0, 0)
        if tick in (2, 4, 6, 8):
            reduce_step(0, tick // 2)
        if 4 <= tick < 4 + n_h:
            split_h(tick - 4)

    gather(0, first_extra)

    def block_rows(ph, s, b):
        flat = cols.at[ph, s].reshape(local_rows, B)
        return flat[pl.ds(b * B, B)]

    for b in range(blocks):
        for s in range(2):
            at = pl.ds((2 * b + s) * B, B)
            hi, lo = halves(block_rows(0, s, b))
            vw[at, :B] = hi
            vw[at, B:] = lo
            zhi_ref[at, :B] = hi
            zlo_ref[at, :B] = lo

    order = (2, 1, -1, 0)
    two_rows = 2 * piece

    def sum_pair(j):
        piece_wait(sib_in.at[j], sib_recv.at[j])
        total = own[j] + sib_in[j]
        ring_out[j] = total
        if order[j]:
            remote(ring_out.at[j], ring_in.at[j], ring_send.at[j], ring_recv.at[j], at_y(order[j])).start()

    for j, off in enumerate(order):
        start = pl.multiple_of(mod4(y + off) * two_rows, 32)
        take = pl.ds(start, two_rows)
        both = dot1(hhi[take], vw[...]) + dot1(hlo[take], vw[...])
        acc[...] = both[:, :B] + both[:, B:]
        mine = pl.ds(pl.multiple_of(core * piece, 8), piece)
        theirs = pl.ds(pl.multiple_of((1 - core) * piece, 8), piece)
        own[j] = acc[mine]
        ring_out[4 + j] = acc[theirs]
        remote(ring_out.at[4 + j], sib_in.at[j], sib_send.at[j], sib_recv.at[j], (row, other)).start()
        if j:
            sum_pair(j - 1)
    sum_pair(3)
    p_piece = ring_out[3]
    for j in range(3):
        piece_wait(ring_in.at[j], ring_recv.at[j])
        p_piece = p_piece + ring_in[j]
    rows[1, col] = p_piece

    eye_r = lax.broadcasted_iota(jnp.int32, (B, B), 0)
    eye_c = lax.broadcasted_iota(jnp.int32, (B, B), 1)
    gram = arout.at[0]

    def inverse_step(i):
        if i == 0:
            g = gram[...]
            half = jnp.sum(jnp.where(eye_r == eye_c, g, 0.0), axis=1, keepdims=True) * 0.5
            start = -(jnp.where(eye_c > eye_r, g, 0.0) / half)
            inverse[...] = start + jnp.where(eye_r == eye_c, 1.0, 0.0)
            power[...] = dot6(start, start)
        elif i < 7:
            now = power[...]
            inverse[...] = inverse[...] + dot6(inverse[...], now)
            if i < 6:
                power[...] = dot6(now, now)
        else:
            g = gram[...]
            half = jnp.sum(jnp.where(eye_r == eye_c, g, 0.0), axis=0, keepdims=True) * 0.5
            inverse[...] = inverse[...] / half

    def second_extra(tick):
        if tick == 0:
            part[1] = dot6(rows[0, col], rows[1, col], TN)
            reduce_step(1, 0)
        if tick in (2, 4, 6, 8):
            reduce_step(1, tick // 2)
        if 1 <= tick < 9:
            inverse_step(tick - 1)

    gather(1, second_extra)

    u = inverse[...]
    middle = dot6(dot6(u, arout[1], TN), u)
    middle = -0.5 * (middle + middle.T)
    v_rows = rows.at[0].reshape(local_rows, B)
    p_rows = rows.at[1].reshape(local_rows, B)
    chunk = 384
    for t in range(local_rows // chunk):
        at = pl.ds(t * chunk, chunk)
        v, p = v_rows[at], p_rows[at]
        hi, lo = halves(dot6(p, u) + dot6(v, middle))
        whi_ref[at, :B] = hi
        wlo_ref[at, :B] = lo
        hi, lo = halves(dot6(v, u, NT))
        whi_ref[at, B:] = hi
        wlo_ref[at, B:] = lo
    for b in range(blocks):
        for s in range(2):
            at = pl.ds((2 * b + s) * B, B)
            hi, lo = halves(block_rows(1, s, b))
            zhi_ref[at, B:] = hi
            zlo_ref[at, B:] = lo

    for ph in range(2):
        gather_finish(ph)
        reduce_finish(ph)
    for j in range(4):
        piece_wait(sib_in.at[j], sib_send.at[j])
    for j in range(3):
        piece_wait(ring_in.at[j], ring_send.at[j])


def update_kernel(h_ref, whi_ref, wlo_ref, zhi_ref, zlo_ref, out_ref):
    zhi = zhi_ref[...]
    change = dot1(whi_ref[...], zhi, NT) + dot1(wlo_ref[...], zhi, NT) + dot1(whi_ref[...], zlo_ref[...], NT)
    out_ref[...] = h_ref[...] - change


def body(hamiltonian, panel):
    m, n = hamiltonian.shape
    piece = panel.shape[0]
    vmem = pl.BlockSpec(memory_space=pltpu.VMEM)
    dma = pltpu.SemaphoreType.DMA
    n_h = 8
    whi, wlo, zhi, zlo = pl.pallas_call(
        panel_kernel,
        out_shape=[
            jax.ShapeDtypeStruct((m, 2 * B), BF16),
            jax.ShapeDtypeStruct((m, 2 * B), BF16),
            jax.ShapeDtypeStruct((n, 2 * B), BF16),
            jax.ShapeDtypeStruct((n, 2 * B), BF16),
        ],
        in_specs=[pl.BlockSpec(memory_space=pl.ANY), vmem],
        out_specs=[vmem] * 4,
        scratch_shapes=[
            pltpu.VMEM((m, n), F32),
            pltpu.VMEM((m, n), BF16),
            pltpu.VMEM((m, n), BF16),
            pltpu.VMEM((n, 2 * B), BF16),
            pltpu.VMEM((2, C, piece, B), F32),
            pltpu.VMEM((2, 2, C, piece, B), F32),
            pltpu.VMEM((2 * piece, B), F32),
            pltpu.VMEM((4, piece, B), F32),
            pltpu.VMEM((4, piece, B), F32),
            pltpu.VMEM((3, piece, B), F32),
            pltpu.VMEM((8, piece, B), F32),
            pltpu.VMEM((2, B, B), F32),
            pltpu.VMEM((2, C, 16, B), F32),
            pltpu.VMEM((2, 4, 16, B), F32),
            pltpu.VMEM((2, 4, 16, B), F32),
            pltpu.VMEM((2, B, B), F32),
            pltpu.VMEM((B, B), F32),
            pltpu.VMEM((B, B), F32),
            dma((n_h,)),
            dma((2, 7)),
            dma((2, C)),
            dma((2, 4, 2, 4)),
            dma((2, 2, C)),
            dma((4,)),
            dma((4,)),
            dma((3,)),
            dma((3,)),
            dma((2, 4)),
            dma((2, 4)),
        ],
        compiler_params=pltpu.CompilerParams(
            collective_id=0, has_side_effects=True, vmem_limit_bytes=50 * 2**20
        ),
        cost_estimate=pl.CostEstimate(flops=4 * m * n * B, bytes_accessed=4 * m * n, transcendentals=0),
        name="panel_products",
    )(hamiltonian, panel)
    tile = 2 * B
    whole = pl.BlockSpec((m, 2 * B), lambda t: (0, 0))
    strip = pl.BlockSpec((tile, 2 * B), lambda t: (t, 0))
    tall = pl.BlockSpec((m, tile), lambda t: (0, t))
    return pl.pallas_call(
        update_kernel,
        out_shape=jax.ShapeDtypeStruct((m, n), F32),
        grid=(n // tile,),
        in_specs=[tall, whole, whole, strip, strip],
        out_specs=tall,
        compiler_params=pltpu.CompilerParams(vmem_limit_bytes=40 * 2**20),
        cost_estimate=pl.CostEstimate(flops=12 * m * n * B, bytes_accessed=8 * m * n, transcendentals=0),
        name="rank_update",
    )(hamiltonian, whi, wlo, zhi, zlo)


def solution(mesh):
    return jax.shard_map(
        body,
        mesh=mesh,
        in_specs=(P("row", "col"), P(("row", "col"), None)),
        out_specs=P("row", "col"),
        check_vma=False,
    )
```

```python
import jax
import jax.numpy as jnp
from jax import lax
from jax.experimental import pallas as pl
from jax.experimental.pallas import tpu as pltpu
from jax.sharding import PartitionSpec as P

B = 128
R = 16
C = 8
MESH = pl.DeviceIdType.MESH
F32 = jnp.float32
BF16 = jnp.bfloat16
HIGHEST = lax.Precision.HIGHEST
NN = (((1,), (0,)), ((), ()))
NT = (((1,), (1,)), ((), ()))
TN = (((0,), (0,)), ((), ()))


def dot6(a, b, dims=NN):
    return lax.dot_general(a, b, dims, precision=HIGHEST, preferred_element_type=F32)


def dot1(a, b, dims=NN):
    return lax.dot_general(a, b, dims, preferred_element_type=F32)


def halves(v):
    hi = v.astype(BF16)
    return hi, (v - hi.astype(F32)).astype(BF16)


def mod4(v):
    return lax.rem(v + 8, 4)


def panel_kernel(
    h_ref, panel_ref, out_ref,
    hhi, hlo, vw, whi, wlo, zhi, zlo, rows, cols, acc, own, sib_in, ring_in, ring_out,
    part, ar1, ar2, arout, power, inverse,
    h_sem, ysend, yrecv, lsend, psend, precv, sib_send, sib_recv, ring_send, ring_recv, ar_send, ar_recv,
):
    row = lax.axis_index("row")
    col = lax.axis_index("col")
    x, z = row // 4, lax.rem(row, 4)
    y, core = col // 2, lax.rem(col, 2)
    other = col + 1 - 2 * core
    piece = panel_ref.shape[0]
    local_rows = out_ref.shape[0]
    blocks = local_rows // B

    def at_y(off):
        return (row, mod4(y + off) * 2 + core)

    line_peers = [(row, lax.rem(col + o, C)) for o in range(1, C)]
    plane_peers = [(lax.rem(row + o, R), col) for o in range(1, R)]

    sign = 1 - 2 * core
    z0 = 2 * lax.rem(y, 2) + core
    x0s = [y // 2, y // 2 + 2]
    dz = mod4((z - z0) * sign)
    dxs = [mod4(x - x0) for x0 in x0s]
    roots = [(dx == 0) & (dz == 0) for dx in dxs]
    OFFS = (0, -1, 1, 2)

    def natural(kk):
        return mod4(y + OFFS[kk // 2]) * 2 + (core if kk % 2 == 0 else 1 - core)

    def place(kk, s):
        p, q = (dz, dxs[s]) if kk & 1 else (dxs[s], dz)
        p = mod4(-p) if (kk >> 1) & 1 else p
        q = mod4(-q) if (kk >> 2) & 1 else q
        return 4 * p + q

    def helper(code):
        return (code == 15) | (code == 6) | (code == 9)

    def neighbour(along_z, step):
        if along_z:
            return (x * 4 + mod4(z + step * sign), col)
        return (mod4(x + step) * 4 + z, col)

    y_to = lax.rem(row, C) // 2
    core_to = lax.rem(z, 2)
    col_to = y_to * 2 + core_to
    off_to = mod4(y - y_to)
    index_to = jnp.where(off_to == 0, 0, jnp.where(off_to == 3, 1, jnp.where(off_to == 1, 2, 3)))
    swap_to = core != core_to
    flip_p = lax.rem(index_to, 2) == 1
    flip_q = index_to >= 2
    helpers_to = []
    for p, q in ((3, 3), (1, 2), (2, 1)):
        p = jnp.where(flip_p, 4 - p, p)
        q = jnp.where(flip_q, 4 - q, q)
        dx_to = jnp.where(swap_to, q, p)
        dz_to = jnp.where(swap_to, p, q)
        helpers_to.append((mod4(x + dx_to) * 4 + mod4(z + dz_to * (1 - 2 * core_to)), col_to))

    barrier = pltpu.get_barrier_semaphore()
    for peer in line_peers + plane_peers:
        pl.semaphore_signal(barrier, inc=1, device_id=peer, device_id_type=MESH)
    for kk in range(8):
        for s in range(2):
            @pl.when(helper(place(kk, s)))
            def _():
                pl.semaphore_signal(
                    barrier, inc=1, device_id=(x0s[s] * 4 + z0, natural(kk)), device_id_type=MESH
                )

    n_h = h_sem.shape[0]
    h_rows = local_rows // n_h
    h_copies = [
        pltpu.make_async_copy(
            h_ref.at[pl.ds(i * h_rows, h_rows)], out_ref.at[pl.ds(i * h_rows, h_rows)], h_sem.at[i]
        )
        for i in range(n_h)
    ]
    for copy in h_copies:
        copy.start()

    position = col * piece + lax.broadcasted_iota(jnp.int32, (piece, B), 0)
    column = lax.broadcasted_iota(jnp.int32, (piece, B), 1)
    global_block = (position >> 7) * R + row
    within = position & (B - 1)
    raw = panel_ref[...]
    unit = jnp.where(column < within, raw, jnp.where(column == within, 1.0, 0.0))
    kept = jnp.where(global_block == 1, unit, 0.0)
    rows[0, col] = jnp.where(global_block >= 2, raw, kept)

    pl.semaphore_wait(barrier, len(line_peers) + len(plane_peers) + 3)

    def remote(src, dst, send, recv, peer):
        return pltpu.make_async_remote_copy(
            src_ref=src, dst_ref=dst, send_sem=send, recv_sem=recv, device_id=peer, device_id_type=MESH
        )

    def wait_for(ref, sem):
        pltpu.make_async_copy(ref, ref, sem).wait()

    mine16 = pl.ds(pl.multiple_of(col * 16, 16), 16)

    def reduce_step(ph, step):
        if step == 0:
            for peer in line_peers:
                remote(
                    part.at[ph, pl.ds(pl.multiple_of(peer[1] * 16, 16), 16)], ar1.at[ph, col],
                    ar_send.at[ph, 0], ar_recv.at[ph, 0], peer,
                ).start()
            ar1[ph, col] = part[ph, mine16]
        elif step == 1:
            wait_for(ar1.at[ph, pl.ds(0, C - 1)], ar_recv.at[ph, 0])
            ar2[ph, row] = sum(ar1[ph, i] for i in range(C))
            for peer in plane_peers:
                remote(ar2.at[ph, row], ar2.at[ph, row], ar_send.at[ph, 1], ar_recv.at[ph, 1], peer).start()
        elif step == 2:
            wait_for(ar2.at[ph, pl.ds(0, R - 1)], ar_recv.at[ph, 1])
            arout[ph, mine16] = sum(ar2[ph, i] for i in range(R))
            for peer in line_peers:
                remote(arout.at[ph, mine16], arout.at[ph, mine16], ar_send.at[ph, 2], ar_recv.at[ph, 2], peer).start()
        else:
            wait_for(arout.at[ph, pl.ds(0, 16 * (C - 1))], ar_recv.at[ph, 2])

    def reduce_finish(ph):
        wait_for(ar1.at[ph, pl.ds(0, C - 1)], ar_send.at[ph, 0])
        wait_for(ar2.at[ph, pl.ds(0, R - 1)], ar_send.at[ph, 1])
        wait_for(ar1.at[ph, pl.ds(0, C - 1)], ar_send.at[ph, 2])

    def line_step(ph, kk):
        k = natural(kk)
        here = rows.at[ph, k]
        if kk == 0:
            for n, off in enumerate((1, -1, 2)):
                remote(here, here, ysend.at[ph, n], yrecv.at[ph, k], at_y(off)).start()
            remote(here, here, ysend.at[ph, 3], yrecv.at[ph, k], (row, other)).start()
            for peer in helpers_to:
                remote(here, cols.at[ph, x // 2, k], lsend.at[ph], precv.at[ph, x // 2, k], peer).start()
        else:
            wait_for(here, yrecv.at[ph, k])
            if kk % 2 == 0:
                remote(here, here, ysend.at[ph, 3 + kk // 2], yrecv.at[ph, k], (row, other)).start()

    def plane_step(ph, kk):
        k = natural(kk)
        swap = kk & 1
        sp = -1 if (kk >> 1) & 1 else 1
        sq = -1 if (kk >> 2) & 1 else 1
        for s in range(2):
            code = place(kk, s)
            here = cols.at[ph, s, k]

            def send(source):
                toward = jnp.where((code == 0) | (code == 9), sp, -sp)
                for peer in (neighbour(not swap, sq), neighbour(not swap, -sq), neighbour(swap, toward)):
                    remote(source, here, psend.at[ph, s, kk], precv.at[ph, s, k], peer).start()

            @pl.when(roots[s])
            def _():
                send(rows.at[ph, k])

            @pl.when(helper(code))
            def _():
                wait_for(here, precv.at[ph, s, k])
                send(here)

    def gather(ph, extra):
        for tick, kk in enumerate((0, 1, 2, 4, 3, 5, 6, 7)):
            line_step(ph, kk)
            plane_step(ph, kk)
            extra(tick)

    def gather_wait(ph):
        for s in range(2):
            for kk in range(8):
                k = natural(kk)
                code = place(kk, s)
                @pl.when(jnp.logical_not(helper(code) | (code == 0)))
                def _():
                    wait_for(cols.at[ph, s, k], precv.at[ph, s, k])
            @pl.when(roots[s])
            def _():
                cols[ph, s] = rows[ph]

    def gather_finish(ph):
        for n in range(7):
            wait_for(rows.at[ph, 0], ysend.at[ph, n])
        three = cols.at[ph, 0, pl.ds(0, 3)]
        wait_for(three, lsend.at[ph])
        for kk in range(8):
            for s in range(2):
                code = place(kk, s)
                @pl.when(helper(code) | (code == 0))
                def _():
                    wait_for(three, psend.at[ph, s, kk])

    def split_h(i):
        h_copies[i].wait()
        hi, lo = halves(out_ref[pl.ds(i * h_rows, h_rows)])
        hhi[pl.ds(i * h_rows, h_rows)] = hi
        hlo[pl.ds(i * h_rows, h_rows)] = lo

    def first_extra(tick):
        if tick == 0:
            part[0] = dot6(rows[0, col], rows[0, col], TN)
            reduce_step(0, 0)
        if tick == 5:
            reduce_step(0, 1)
        split_h(tick)

    gather(0, first_extra)
    gather_wait(0)
    reduce_step(0, 2)

    def block_rows(ph, s, b):
        flat = cols.at[ph, s].reshape(local_rows, B)
        return flat[pl.ds(b * B, B)]

    for b in range(blocks):
        for s in range(2):
            at = pl.ds((2 * b + s) * B, B)
            hi, lo = halves(block_rows(0, s, b))
            vw[at, :B] = hi
            vw[at, B:] = lo
            zhi[at, :B] = hi
            zlo[at, :B] = lo

    order = (2, 1, -1, 0)
    two_rows = 2 * piece
    v_rows = rows.at[0].reshape(local_rows, B)
    p_rows = rows.at[1].reshape(local_rows, B)

    def sum_pair(j):
        wait_for(sib_in.at[j], sib_recv.at[j])
        ring_out[j] = own[j] + sib_in[j]
        if order[j]:
            remote(ring_out.at[j], ring_in.at[j], ring_send.at[j], ring_recv.at[j], at_y(order[j])).start()

    for j, off in enumerate(order):
        take = pl.ds(pl.multiple_of(mod4(y + off) * two_rows, 32), two_rows)
        both = dot1(hhi[take], vw[...]) + dot1(hlo[take], vw[...])
        acc[...] = both[:, :B] + both[:, B:]
        mine = pl.ds(pl.multiple_of(core * piece, 8), piece)
        theirs = pl.ds(pl.multiple_of((1 - core) * piece, 8), piece)
        own[j] = acc[mine]
        ring_out[4 + j] = acc[theirs]
        remote(ring_out.at[4 + j], sib_in.at[j], sib_send.at[j], sib_recv.at[j], (row, other)).start()
        cross = dot6(v_rows[take], acc[...], TN)
        part[1] = cross if j == 0 else part[1] + cross
        if j:
            sum_pair(j - 1)
    sum_pair(3)
    reduce_step(1, 0)
    p_piece = ring_out[3]
    for j in range(3):
        wait_for(ring_in.at[j], ring_recv.at[j])
        p_piece = p_piece + ring_in[j]
    rows[1, col] = p_piece

    eye_r = lax.broadcasted_iota(jnp.int32, (B, B), 0)
    eye_c = lax.broadcasted_iota(jnp.int32, (B, B), 1)
    gram = arout.at[0]

    def inverse_step(i):
        if i == 0:
            g = gram[...]
            half = jnp.sum(jnp.where(eye_r == eye_c, g, 0.0), axis=1, keepdims=True) * 0.5
            start = -(jnp.where(eye_c > eye_r, g, 0.0) / half)
            inverse[...] = start + jnp.where(eye_r == eye_c, 1.0, 0.0)
            power[...] = dot6(start, start)
        elif i < 7:
            now = power[...]
            inverse[...] = inverse[...] + dot6(inverse[...], now)
            if i < 6:
                power[...] = dot6(now, now)
        else:
            g = gram[...]
            half = jnp.sum(jnp.where(eye_r == eye_c, g, 0.0), axis=0, keepdims=True) * 0.5
            inverse[...] = inverse[...] / half

    def second_extra(tick):
        if tick == 0:
            reduce_step(1, 1)
            reduce_step(0, 3)
        if tick == 5:
            reduce_step(1, 2)
        inverse_step(tick)

    gather(1, second_extra)
    reduce_step(1, 3)

    u = inverse[...]
    middle = dot6(dot6(u, arout[1], TN), u)
    middle = -0.5 * (middle + middle.T)
    chunk = 384
    for t in range(local_rows // chunk):
        at = pl.ds(t * chunk, chunk)
        v, p = v_rows[at], p_rows[at]
        hi, lo = halves(dot6(p, u) + dot6(v, middle))
        whi[at, :B] = hi
        wlo[at, :B] = lo
        hi, lo = halves(dot6(v, u, NT))
        whi[at, B:] = hi
        wlo[at, B:] = lo

    gather_wait(1)
    for b in range(blocks):
        for s in range(2):
            at = pl.ds((2 * b + s) * B, B)
            hi, lo = halves(block_rows(1, s, b))
            zhi[at, B:] = hi
            zlo[at, B:] = lo

    def update(b, carry):
        at = pl.ds(pl.multiple_of(b * 2 * B, 2 * B), 2 * B)
        high = zhi[at]
        change = dot1(whi[...], high, NT) + dot1(wlo[...], high, NT) + dot1(whi[...], zlo[at], NT)
        out_ref[:, at] = out_ref[:, at] - change
        return carry

    lax.fori_loop(0, blocks, update, 0)

    for ph in range(2):
        gather_finish(ph)
        reduce_finish(ph)
    for j in range(4):
        wait_for(sib_in.at[j], sib_send.at[j])
    for j in range(3):
        wait_for(ring_in.at[j], ring_send.at[j])


def body(hamiltonian, panel):
    m, n = hamiltonian.shape
    piece = panel.shape[0]
    vmem = pl.BlockSpec(memory_space=pltpu.VMEM)
    dma = pltpu.SemaphoreType.DMA
    return pl.pallas_call(
        panel_kernel,
        out_shape=jax.ShapeDtypeStruct((m, n), F32),
        in_specs=[pl.BlockSpec(memory_space=pl.ANY), vmem],
        out_specs=vmem,
        scratch_shapes=[
            pltpu.VMEM((m, n), BF16),
            pltpu.VMEM((m, n), BF16),
            pltpu.VMEM((n, 2 * B), BF16),
            pltpu.VMEM((m, 2 * B), BF16),
            pltpu.VMEM((m, 2 * B), BF16),
            pltpu.VMEM((n, 2 * B), BF16),
            pltpu.VMEM((n, 2 * B), BF16),
            pltpu.VMEM((2, C, piece, B), F32),
            pltpu.VMEM((2, 2, C, piece, B), F32),
            pltpu.VMEM((2 * piece, B), F32),
            pltpu.VMEM((4, piece, B), F32),
            pltpu.VMEM((4, piece, B), F32),
            pltpu.VMEM((3, piece, B), F32),
            pltpu.VMEM((8, piece, B), F32),
            pltpu.VMEM((2, B, B), F32),
            pltpu.VMEM((2, C, 16, B), F32),
            pltpu.VMEM((2, R, 16, B), F32),
            pltpu.VMEM((2, B, B), F32),
            pltpu.VMEM((B, B), F32),
            pltpu.VMEM((B, B), F32),
            dma((8,)),
            dma((2, 7)),
            dma((2, C)),
            dma((2,)),
            dma((2, 2, C)),
            dma((2, 2, C)),
            dma((4,)),
            dma((4,)),
            dma((3,)),
            dma((3,)),
            dma((2, 3)),
            dma((2, 3)),
        ],
        compiler_params=pltpu.CompilerParams(
            collective_id=0, has_side_effects=True, vmem_limit_bytes=40 * 2**20
        ),
        cost_estimate=pl.CostEstimate(flops=16 * m * n * B, bytes_accessed=4 * m * n, transcendentals=0),
        name="panel_update",
    )(hamiltonian, panel)


def solution(mesh):
    return jax.shard_map(
        body,
        mesh=mesh,
        in_specs=(P("row", "col"), P(("row", "col"), None)),
        out_specs=P("row", "col"),
        check_vma=False,
    )
```

```python
import jax
import jax.numpy as jnp
from jax import lax
from jax.experimental import pallas as pl
from jax.experimental.pallas import tpu as pltpu
from jax.sharding import PartitionSpec as P

B = 128
R = 16
C = 8
MESH = pl.DeviceIdType.MESH
F32 = jnp.float32
BF16 = jnp.bfloat16
HIGHEST = lax.Precision.HIGHEST

PATTERNS = (
    ((0, 14, 7, 3), ((1, 8, 12), (13, 10, 9), (6, 11, 4), (2, 5, 15))),
    ((0, 7, 4, 14), ((3, 1, 12), (10, 6, 11), (8, 9, 5), (15, 2, 13))),
    ((0, 2, 12, 11), ((4, 5, 3), (1, 14, 6), (9, 13, 8), (7, 15, 10))),
    ((0, 14, 7, 3), ((1, 5, 12), (13, 10, 9), (4, 6, 11), (2, 8, 15))),
    ((0, 3, 13, 11), ((1, 4, 12), (7, 2, 6), (14, 9, 5), (15, 8, 10))),
    ((0, 14, 7, 3), ((8, 4, 12), (13, 10, 9), (6, 11, 5), (2, 1, 15))),
    ((0, 3, 4, 10), ((1, 12, 13), (15, 2, 14), (7, 5, 8), (9, 11, 6))),
    ((0, 14, 7, 3), ((1, 8, 12), (13, 10, 9), (6, 11, 4), (2, 5, 15))),
)
NN = (((1,), (0,)), ((), ()))
NT = (((1,), (1,)), ((), ()))
TN = (((0,), (0,)), ((), ()))


def dot6(a, b, dims=NN):
    return lax.dot_general(a, b, dims, precision=HIGHEST, preferred_element_type=F32)


def dot1(a, b, dims=NN):
    return lax.dot_general(a, b, dims, preferred_element_type=F32)


def halves(v):
    hi = v.astype(BF16)
    return hi, (v - hi.astype(F32)).astype(BF16)


def mod4(v):
    return lax.rem(v + 8, 4)


def panel_kernel(
    h_ref, panel_ref, h_out, whi, wlo, zhi, zlo,
    hhi, hlo, vw, rows, cols, acc, sib_in, ring_in, ring_out, raw_panel,
    part, ar1, ar2, arout, power, inverse,
    p_sem, h_sem, ysend, yrecv, lsend, psend, precv, sib_send, sib_recv, ring_send, ring_recv, ar_send, ar_recv,
):
    row = lax.axis_index("row")
    col = lax.axis_index("col")
    x, z = row // 4, lax.rem(row, 4)
    y, core = col // 2, lax.rem(col, 2)
    other = col + 1 - 2 * core
    panel_copy = pltpu.make_async_copy(panel_ref, raw_panel, p_sem)
    panel_copy.start()
    piece = panel_ref.shape[0]
    local_rows = h_out.shape[0]
    blocks = local_rows // B

    def at_y(off):
        return (row, mod4(y + off) * 2 + core)

    line_peers = [(row, lax.rem(col + o, C)) for o in range(1, C)]
    plane_peers = [(lax.rem(row + o, R), col) for o in range(1, R)]

    sz = 1 - 2 * core
    sx = 1 - 2 * (y // 2)
    z0 = 2 * lax.rem(y, 2) + core
    x0s = [y // 2, y // 2 + 2]
    codes = [4 * mod4((x - x0) * sx) + mod4((z - z0) * sz) for x0 in x0s]
    roots = [code == 0 for code in codes]
    OFFS = (0, -1, 1, 2)

    def natural(kk):
        return mod4(y + OFFS[kk // 2]) * 2 + (core if kk % 2 == 0 else 1 - core)

    def chain(key, keys, values):
        out = values[0]
        for k, v in zip(keys[1:], values[1:]):
            out = jnp.where(key == k, v, out)
        return out

    def helper(kk, s):
        first, second, third = PATTERNS[kk][0][1:]
        return (codes[s] == first) | (codes[s] == second) | (codes[s] == third)

    def next_chips(kk, s):
        heads, groups = PATTERNS[kk]
        for n in range(3):
            steps = [
                4 * ((group[n] // 4 - head // 4) % 4) + (group[n] % 4 - head % 4) % 4
                for head, group in zip(heads, groups)
            ]
            step = chain(codes[s], heads, steps)
            yield (mod4(x + sx * (step // 4)) * 4 + mod4(z + sz * lax.rem(step, 4)), col)

    y_to = lax.rem(row, C) // 2
    core_to = lax.rem(z, 2)
    col_to = y_to * 2 + core_to
    off_to = mod4(y - y_to)
    index_to = jnp.where(off_to == 0, 0, jnp.where(off_to == 3, 1, jnp.where(off_to == 1, 2, 3)))
    kk_to = 2 * index_to + jnp.where(core == core_to, 0, 1)
    sx_to = 1 - 2 * (y_to // 2)
    sz_to = 1 - 2 * core_to
    helpers_to = []
    for n in range(1, 4):
        step = chain(kk_to, range(8), [heads[n] for heads, _ in PATTERNS])
        helpers_to.append((mod4(x + sx_to * (step // 4)) * 4 + mod4(z + sz_to * lax.rem(step, 4)), col_to))

    barrier = pltpu.get_barrier_semaphore()
    for peer in line_peers + plane_peers:
        pl.semaphore_signal(barrier, inc=1, device_id=peer, device_id_type=MESH)
    for kk in range(8):
        for s in range(2):
            @pl.when(helper(kk, s))
            def _():
                pl.semaphore_signal(
                    barrier, inc=1, device_id=(x0s[s] * 4 + z0, natural(kk)), device_id_type=MESH
                )

    n_h = h_sem.shape[0]
    h_rows = local_rows // n_h
    h_copies = [
        pltpu.make_async_copy(
            h_ref.at[pl.ds(i * h_rows, h_rows)], h_out.at[pl.ds(i * h_rows, h_rows)], h_sem.at[i]
        )
        for i in range(n_h)
    ]
    for copy in h_copies:
        copy.start()

    position = col * piece + lax.broadcasted_iota(jnp.int32, (piece, B), 0)
    column = lax.broadcasted_iota(jnp.int32, (piece, B), 1)
    global_block = (position >> 7) * R + row
    within = position & (B - 1)
    panel_copy.wait()
    raw = raw_panel[...]
    unit = jnp.where(column < within, raw, jnp.where(column == within, 1.0, 0.0))
    kept = jnp.where(global_block == 1, unit, 0.0)
    rows[0, col] = jnp.where(global_block >= 2, raw, kept)

    pl.semaphore_wait(barrier, len(line_peers) + len(plane_peers) + 3)

    def remote(src, dst, send, recv, peer):
        return pltpu.make_async_remote_copy(
            src_ref=src, dst_ref=dst, send_sem=send, recv_sem=recv, device_id=peer, device_id_type=MESH
        )

    def wait_for(ref, sem):
        pltpu.make_async_copy(ref, ref, sem).wait()

    mine16 = pl.ds(pl.multiple_of(col * 16, 16), 16)

    def reduce_step(ph, step):
        if step == 0:
            for peer in line_peers:
                remote(
                    part.at[ph, pl.ds(pl.multiple_of(peer[1] * 16, 16), 16)], ar1.at[ph, col],
                    ar_send.at[ph, 0], ar_recv.at[ph, 0], peer,
                ).start()
            ar1[ph, col] = part[ph, mine16]
        elif step == 1:
            wait_for(ar1.at[ph, pl.ds(0, C - 1)], ar_recv.at[ph, 0])
            ar2[ph, row] = sum(ar1[ph, i] for i in range(C))
            for peer in plane_peers:
                remote(ar2.at[ph, row], ar2.at[ph, row], ar_send.at[ph, 1], ar_recv.at[ph, 1], peer).start()
        elif step == 2:
            wait_for(ar2.at[ph, pl.ds(0, R - 1)], ar_recv.at[ph, 1])
            arout[ph, mine16] = sum(ar2[ph, i] for i in range(R))
            for peer in line_peers:
                remote(arout.at[ph, mine16], arout.at[ph, mine16], ar_send.at[ph, 2], ar_recv.at[ph, 2], peer).start()
        else:
            wait_for(arout.at[ph, pl.ds(0, 16 * (C - 1))], ar_recv.at[ph, 2])

    def reduce_finish(ph):
        wait_for(ar1.at[ph, pl.ds(0, C - 1)], ar_send.at[ph, 0])
        wait_for(ar2.at[ph, pl.ds(0, R - 1)], ar_send.at[ph, 1])
        wait_for(ar1.at[ph, pl.ds(0, C - 1)], ar_send.at[ph, 2])

    am_root = col == col_to
    other_root = other == col_to
    OTHERS = (1, -1, 2)

    def other_is_root(off):
        return (mod4(y + off) == y_to) & (core == core_to)

    def first_sends(ph):
        here = rows.at[ph, col]
        @pl.when(jnp.logical_not(am_root))
        def _():
            remote(here, here, ysend.at[ph, 0], yrecv.at[ph, col], (row, col_to)).start()
        for peer in helpers_to:
            remote(here, cols.at[ph, x // 2, col], lsend.at[ph], precv.at[ph, x // 2, col], peer).start()

    def line_start(ph):
        here = rows.at[ph, col]
        for n, off in enumerate(OTHERS):
            @pl.when(jnp.logical_not(other_is_root(off)))
            def _():
                remote(here, here, ysend.at[ph, 1 + n], yrecv.at[ph, col], at_y(off)).start()
        @pl.when(jnp.logical_not(other_root))
        def _():
            remote(here, here, ysend.at[ph, 4], yrecv.at[ph, col], (row, other)).start()

    def line_step(ph, kk):
        k = natural(kk)
        here = rows.at[ph, k]
        @pl.when(jnp.logical_not(am_root))
        def _():
            wait_for(here, yrecv.at[ph, k])
        if kk % 2 == 0:
            @pl.when(jnp.logical_not(other_root))
            def _():
                remote(here, here, ysend.at[ph, 4 + kk // 2], yrecv.at[ph, k], (row, other)).start()

    def plane_step(ph, kk):
        k = natural(kk)
        for s in range(2):
            here = cols.at[ph, s, k]

            def send(source):
                for peer in next_chips(kk, s):
                    remote(source, here, psend.at[ph, s, kk], precv.at[ph, s, k], peer).start()

            @pl.when(roots[s])
            def _():
                if kk:
                    wait_for(rows.at[ph, k], yrecv.at[ph, k])
                send(rows.at[ph, k])

            @pl.when(helper(kk, s))
            def _():
                wait_for(here, precv.at[ph, s, k])
                send(here)

    ORDER = (0, 1, 2, 4, 3, 5, 6, 7)

    def gather(ph, extra):
        first_sends(ph)
        for tick, kk in enumerate(ORDER):
            plane_step(ph, kk)
            if tick == 4:
                line_start(ph)
            extra(tick)

    def gather_wait(ph):
        for s in range(2):
            for kk in range(8):
                k = natural(kk)
                @pl.when(jnp.logical_not(helper(kk, s) | roots[s]))
                def _():
                    wait_for(cols.at[ph, s, k], precv.at[ph, s, k])
            @pl.when(roots[s])
            def _():
                cols[ph, s] = rows[ph]

    def gather_finish(ph):
        sent = [jnp.logical_not(am_root)] + [jnp.logical_not(other_is_root(off)) for off in OTHERS]
        for n, flag in enumerate(sent + [jnp.logical_not(other_root)] * 4):
            @pl.when(flag)
            def _():
                wait_for(rows.at[ph, 0], ysend.at[ph, n])
        three = cols.at[ph, 0, pl.ds(0, 3)]
        wait_for(three, lsend.at[ph])
        for kk in range(8):
            for s in range(2):
                @pl.when(helper(kk, s) | roots[s])
                def _():
                    wait_for(three, psend.at[ph, s, kk])

    def split_h(i):
        h_copies[i].wait()
        hi, lo = halves(h_out[pl.ds(i * h_rows, h_rows)])
        hhi[pl.ds(i * h_rows, h_rows)] = hi
        hlo[pl.ds(i * h_rows, h_rows)] = lo

    def first_extra(tick):
        if tick == 0:
            part[0] = dot6(rows[0, col], rows[0, col], TN)
            reduce_step(0, 0)
        if tick == 5:
            reduce_step(0, 1)
        split_h(tick)

    gather(0, first_extra)
    gather_wait(0)

    def block_rows(ph, s, b):
        flat = cols.at[ph, s].reshape(local_rows, B)
        return flat[pl.ds(b * B, B)]

    for b in range(blocks):
        for s in range(2):
            at = pl.ds((2 * b + s) * B, B)
            hi, lo = halves(block_rows(0, s, b))
            vw[at, :B] = hi
            vw[at, B:] = lo
            zhi[at, :B] = hi
            zlo[at, :B] = lo

    order = (2, 1, -1, 0)
    two_rows = 2 * piece
    v_rows = rows.at[0].reshape(local_rows, B)
    p_rows = rows.at[1].reshape(local_rows, B)

    def part_of(j, which):
        start = mod4(y + order[j]) * two_rows + which * piece
        return pl.ds(pl.multiple_of(start, 16), piece)

    def sum_pair(j):
        wait_for(sib_in.at[j], sib_recv.at[j])
        ring_out[j] = acc[part_of(j, core)] + sib_in[j]
        if order[j]:
            remote(ring_out.at[j], ring_in.at[j], ring_send.at[j], ring_recv.at[j], at_y(order[j])).start()

    for j, off in enumerate(order):
        take = pl.ds(pl.multiple_of(mod4(y + off) * two_rows, 32), two_rows)
        both = dot1(hhi[take], vw[...]) + dot1(hlo[take], vw[...])
        acc[take] = both[:, :B] + both[:, B:]
        remote(
            acc.at[part_of(j, 1 - core)], sib_in.at[j], sib_send.at[j], sib_recv.at[j], (row, other)
        ).start()
        if j:
            sum_pair(j - 1)
        if j == 2:
            reduce_step(0, 2)
    sum_pair(3)
    for kk in ORDER[1:]:
        line_step(0, kk)
    part[1] = dot6(v_rows[...], acc[...], TN)
    reduce_step(1, 0)
    p_piece = ring_out[3]
    for j in range(3):
        wait_for(ring_in.at[j], ring_recv.at[j])
        p_piece = p_piece + ring_in[j]
    rows[1, col] = p_piece

    eye_r = lax.broadcasted_iota(jnp.int32, (B, B), 0)
    eye_c = lax.broadcasted_iota(jnp.int32, (B, B), 1)
    gram = arout.at[0]

    def inverse_step(i):
        if i == 0:
            g = gram[...]
            half = jnp.sum(jnp.where(eye_r == eye_c, g, 0.0), axis=1, keepdims=True) * 0.5
            start = -(jnp.where(eye_c > eye_r, g, 0.0) / half)
            inverse[...] = start + jnp.where(eye_r == eye_c, 1.0, 0.0)
            power[...] = dot6(start, start)
        elif i < 7:
            now = power[...]
            inverse[...] = inverse[...] + dot6(inverse[...], now)
            if i < 6:
                power[...] = dot6(now, now)
        else:
            g = gram[...]
            half = jnp.sum(jnp.where(eye_r == eye_c, g, 0.0), axis=0, keepdims=True) * 0.5
            inverse[...] = inverse[...] / half

    def second_extra(tick):
        if tick == 0:
            reduce_step(1, 1)
            reduce_step(0, 3)
        if tick == 5:
            reduce_step(1, 2)
        inverse_step(tick)

    gather(1, second_extra)
    for kk in ORDER[1:]:
        line_step(1, kk)
    reduce_step(1, 3)

    u = inverse[...]
    middle = dot6(dot6(u, arout[1], TN), u)
    middle = -0.5 * (middle + middle.T)
    chunk = 384
    for t in range(local_rows // chunk):
        at = pl.ds(t * chunk, chunk)
        v, p = v_rows[at], p_rows[at]
        hi, lo = halves(dot6(p, u) + dot6(v, middle))
        whi[at, :B] = hi
        wlo[at, :B] = lo
        hi, lo = halves(dot6(v, u, NT))
        whi[at, B:] = hi
        wlo[at, B:] = lo

    gather_wait(1)
    for b in range(blocks):
        for s in range(2):
            at = pl.ds((2 * b + s) * B, B)
            hi, lo = halves(block_rows(1, s, b))
            zhi[at, B:] = hi
            zlo[at, B:] = lo

    for ph in range(2):
        gather_finish(ph)
        reduce_finish(ph)
    for j in range(4):
        wait_for(sib_in.at[j], sib_send.at[j])
    for j in range(3):
        wait_for(ring_in.at[j], ring_send.at[j])


def update_kernel(h_ref, whi, wlo, zhi, zlo, out_ref, tiles, sem):
    width = tiles.shape[2]
    slots = tiles.shape[0]
    steps = h_ref.shape[1] // width

    def copy(b):
        slot = lax.rem(b, slots)
        return pltpu.make_async_copy(
            tiles.at[slot], out_ref.at[:, pl.ds(pl.multiple_of(b * width, width), width)], sem.at[slot]
        )

    def step(b, carry):
        @pl.when(b >= slots)
        def _():
            copy(b - slots).wait()

        at = pl.ds(pl.multiple_of(b * width, width), width)
        high = zhi[at]
        change = dot1(whi[...], high, NT) + dot1(wlo[...], high, NT) + dot1(whi[...], zlo[at], NT)
        tiles[lax.rem(b, slots)] = h_ref[:, at] - change
        copy(b).start()
        return carry

    lax.fori_loop(0, steps, step, 0)
    for b in range(steps - slots, steps):
        copy(b).wait()


def body(hamiltonian, panel):
    m, n = hamiltonian.shape
    piece = panel.shape[0]
    vmem = pl.BlockSpec(memory_space=pltpu.VMEM)
    hbm = pl.BlockSpec(memory_space=pl.ANY)
    dma = pltpu.SemaphoreType.DMA
    operands = pl.pallas_call(
        panel_kernel,
        out_shape=[
            jax.ShapeDtypeStruct((m, n), F32),
            jax.ShapeDtypeStruct((m, 2 * B), BF16),
            jax.ShapeDtypeStruct((m, 2 * B), BF16),
            jax.ShapeDtypeStruct((n, 2 * B), BF16),
            jax.ShapeDtypeStruct((n, 2 * B), BF16),
        ],
        in_specs=[hbm, hbm],
        out_specs=[vmem] * 5,
        scratch_shapes=[
            pltpu.VMEM((m, n), BF16),
            pltpu.VMEM((m, n), BF16),
            pltpu.VMEM((n, 2 * B), BF16),
            pltpu.VMEM((2, C, piece, B), F32),
            pltpu.VMEM((2, 2, C, piece, B), F32),
            pltpu.VMEM((m, B), F32),
            pltpu.VMEM((4, piece, B), F32),
            pltpu.VMEM((3, piece, B), F32),
            pltpu.VMEM((4, piece, B), F32),
            pltpu.VMEM((piece, B), F32),
            pltpu.VMEM((2, B, B), F32),
            pltpu.VMEM((2, C, 16, B), F32),
            pltpu.VMEM((2, R, 16, B), F32),
            pltpu.VMEM((2, B, B), F32),
            pltpu.VMEM((B, B), F32),
            pltpu.VMEM((B, B), F32),
            dma,
            dma((8,)),
            dma((2, 8)),
            dma((2, C)),
            dma((2,)),
            dma((2, 2, C)),
            dma((2, 2, C)),
            dma((4,)),
            dma((4,)),
            dma((3,)),
            dma((3,)),
            dma((2, 3)),
            dma((2, 3)),
        ],
        compiler_params=pltpu.CompilerParams(
            collective_id=0, has_side_effects=True, vmem_limit_bytes=40 * 2**20
        ),
        cost_estimate=pl.CostEstimate(flops=8 * m * n * B, bytes_accessed=4 * m * n, transcendentals=0),
        name="panel_products",
    )(hamiltonian, panel)
    return pl.pallas_call(
        update_kernel,
        out_shape=jax.ShapeDtypeStruct((m, n), F32),
        in_specs=[vmem] * 5,
        out_specs=hbm,
        scratch_shapes=[pltpu.VMEM((3, m, 2 * B), F32), dma((3,))],
        compiler_params=pltpu.CompilerParams(vmem_limit_bytes=24 * 2**20),
        cost_estimate=pl.CostEstimate(flops=12 * m * n * B, bytes_accessed=4 * m * n, transcendentals=0),
        name="rank_update",
    )(*operands)


def solution(mesh):
    return jax.shard_map(
        body,
        mesh=mesh,
        in_specs=(P("row", "col"), P(("row", "col"), None)),
        out_specs=P("row", "col"),
        check_vma=False,
    )
```

```python
import jax
import jax.numpy as jnp
from jax import lax
from jax.experimental import pallas as pl
from jax.experimental.pallas import tpu as pltpu
from jax.sharding import PartitionSpec as P

B = 128
R = 16
C = 8
MESH = pl.DeviceIdType.MESH
F32 = jnp.float32
BF16 = jnp.bfloat16
HIGHEST = lax.Precision.HIGHEST

PATTERNS = (
    ((0, 2, 4, 8, 11, 12, 13), ((), (1, 3, 6, 14), (5, 7), (), (10, 15), (), (9,))),
    ((0, 1, 4, 7, 8, 11, 12, 15), ((), (2, 13), (5,), (3, 6), (9,), (10,), (), (14,))),
    ((0, 2, 4, 11, 13), ((3,), (1, 6, 14), (5,), (7, 8, 10, 15), (9, 12))),
    ((0, 5, 7, 8, 14), ((1,), (9,), (3, 4, 6, 11), (12,), (2, 10, 13, 15))),
    ((0, 2, 4, 9, 12), ((), (1, 3, 6, 14), (5, 7, 8), (10, 11, 13), (15,))),
    ((0, 5, 7, 8, 14), ((3,), (1, 9), (4, 6), (11, 12), (2, 10, 13, 15))),
    ((0, 5, 7, 14), ((8, 12), (1, 6, 9, 13), (3, 4, 11), (2, 10, 15))),
    ((0, 9, 10, 15), ((1, 4, 12), (5, 8, 13), (2, 6, 11, 14), (3, 7))),
)
NN = (((1,), (0,)), ((), ()))
NT = (((1,), (1,)), ((), ()))
TN = (((0,), (0,)), ((), ()))


def dot6(a, b, dims=NN):
    return lax.dot_general(a, b, dims, precision=HIGHEST, preferred_element_type=F32)


def dot1(a, b, dims=NN):
    return lax.dot_general(a, b, dims, preferred_element_type=F32)


def halves(v):
    hi = v.astype(BF16)
    return hi, (v - hi.astype(F32)).astype(BF16)


def mod4(v):
    return lax.rem(v + 8, 4)


def panel_kernel(
    h_ref, panel_ref, h_out, whi, wlo, zhi, zlo,
    hhi, hlo, vw, rows, cols, acc, sib_in, ring_in, ring_out, raw_panel,
    part, ar1, ar2, arout, power, inverse,
    p_sem, h_sem, ysend, yrecv, lsend, psend, precv, sib_send, sib_recv, ring_send, ring_recv, ar_send, ar_recv,
):
    row = lax.axis_index("row")
    col = lax.axis_index("col")
    x, z = row // 4, lax.rem(row, 4)
    y, core = col // 2, lax.rem(col, 2)
    other = col + 1 - 2 * core
    panel_copy = pltpu.make_async_copy(panel_ref, raw_panel, p_sem)
    panel_copy.start()
    piece = panel_ref.shape[0]
    local_rows = h_out.shape[0]
    blocks = local_rows // B

    def at_y(off):
        return (row, mod4(y + off) * 2 + core)

    line_peers = [(row, lax.rem(col + o, C)) for o in range(1, C)]
    plane_peers = [(lax.rem(row + o, R), col) for o in range(1, R)]

    sz = 1 - 2 * core
    sx = 1 - 2 * (y // 2)
    z0 = 2 * lax.rem(y, 2) + core
    x0s = [y // 2, y // 2 + 2]
    codes = [4 * mod4((x - x0) * sx) + mod4((z - z0) * sz) for x0 in x0s]
    roots = [code == 0 for code in codes]
    OFFS = (0, -1, 1, 2)

    def natural(kk):
        return mod4(y + OFFS[kk // 2]) * 2 + (core if kk % 2 == 0 else 1 - core)

    def chain(key, keys, values):
        out = values[0]
        for k, v in zip(keys[1:], values[1:]):
            out = jnp.where(key == k, v, out)
        return out

    def among(key, keys):
        found = key == keys[0]
        for k in keys[1:]:
            found = found | (key == k)
        return found

    def helper(kk, s):
        return among(codes[s], PATTERNS[kk][0][1:])

    def next_chips(kk, s):
        heads, groups = PATTERNS[kk]
        for n in range(max(len(group) for group in groups)):
            pairs = [(head, group[n]) for head, group in zip(heads, groups) if len(group) > n]
            keys = [head for head, _ in pairs]
            steps = [4 * ((to // 4 - head // 4) % 4) + (to % 4 - head % 4) % 4 for head, to in pairs]
            step = chain(codes[s], keys, steps)
            peer = (mod4(x + sx * (step // 4)) * 4 + mod4(z + sz * lax.rem(step, 4)), col)
            yield peer, None if len(keys) == len(heads) else among(codes[s], keys)

    def when(flag, act):
        if flag is None:
            act()
        else:
            pl.when(flag)(act)

    y_to = lax.rem(row, C) // 2
    core_to = lax.rem(z, 2)
    col_to = y_to * 2 + core_to
    off_to = mod4(y - y_to)
    index_to = jnp.where(off_to == 0, 0, jnp.where(off_to == 3, 1, jnp.where(off_to == 1, 2, 3)))
    kk_to = 2 * index_to + jnp.where(core == core_to, 0, 1)
    sx_to = 1 - 2 * (y_to // 2)
    sz_to = 1 - 2 * core_to
    counts = [len(heads) - 1 for heads, _ in PATTERNS]
    count_to = chain(kk_to, range(8), counts)
    helpers_to = []
    for n in range(max(counts)):
        having = [kk for kk in range(8) if counts[kk] > n]
        step = chain(kk_to, having, [PATTERNS[kk][0][n + 1] for kk in having])
        peer = (mod4(x + sx_to * (step // 4)) * 4 + mod4(z + sz_to * lax.rem(step, 4)), col_to)
        helpers_to.append((peer, None if len(having) == 8 else count_to > n))

    barrier = pltpu.get_barrier_semaphore()
    for peer in line_peers + plane_peers:
        pl.semaphore_signal(barrier, inc=1, device_id=peer, device_id_type=MESH)
    for kk in range(8):
        for s in range(2):
            @pl.when(helper(kk, s))
            def _():
                pl.semaphore_signal(
                    barrier, inc=1, device_id=(x0s[s] * 4 + z0, natural(kk)), device_id_type=MESH
                )

    n_h = h_sem.shape[0]
    h_rows = local_rows // n_h
    h_copies = [
        pltpu.make_async_copy(
            h_ref.at[pl.ds(i * h_rows, h_rows)], h_out.at[pl.ds(i * h_rows, h_rows)], h_sem.at[i]
        )
        for i in range(n_h)
    ]
    for copy in h_copies:
        copy.start()

    position = col * piece + lax.broadcasted_iota(jnp.int32, (piece, B), 0)
    column = lax.broadcasted_iota(jnp.int32, (piece, B), 1)
    global_block = (position >> 7) * R + row
    within = position & (B - 1)
    panel_copy.wait()
    raw = raw_panel[...]
    unit = jnp.where(column < within, raw, jnp.where(column == within, 1.0, 0.0))
    kept = jnp.where(global_block == 1, unit, 0.0)
    rows[0, col] = jnp.where(global_block >= 2, raw, kept)

    pl.semaphore_wait(barrier, len(line_peers) + len(plane_peers) + count_to)

    def remote(src, dst, send, recv, peer):
        return pltpu.make_async_remote_copy(
            src_ref=src, dst_ref=dst, send_sem=send, recv_sem=recv, device_id=peer, device_id_type=MESH
        )

    def wait_for(ref, sem):
        pltpu.make_async_copy(ref, ref, sem).wait()

    mine16 = pl.ds(pl.multiple_of(col * 16, 16), 16)

    def reduce_step(ph, step):
        if step == 0:
            for peer in line_peers:
                remote(
                    part.at[ph, pl.ds(pl.multiple_of(peer[1] * 16, 16), 16)], ar1.at[ph, col],
                    ar_send.at[ph, 0], ar_recv.at[ph, 0], peer,
                ).start()
            ar1[ph, col] = part[ph, mine16]
        elif step == 1:
            wait_for(ar1.at[ph, pl.ds(0, C - 1)], ar_recv.at[ph, 0])
            ar2[ph, row] = sum(ar1[ph, i] for i in range(C))
            for peer in plane_peers:
                remote(ar2.at[ph, row], ar2.at[ph, row], ar_send.at[ph, 1], ar_recv.at[ph, 1], peer).start()
        elif step == 2:
            wait_for(ar2.at[ph, pl.ds(0, R - 1)], ar_recv.at[ph, 1])
            arout[ph, mine16] = sum(ar2[ph, i] for i in range(R))
            for peer in line_peers:
                remote(arout.at[ph, mine16], arout.at[ph, mine16], ar_send.at[ph, 2], ar_recv.at[ph, 2], peer).start()
        else:
            wait_for(arout.at[ph, pl.ds(0, 16 * (C - 1))], ar_recv.at[ph, 2])

    def reduce_finish(ph):
        wait_for(ar1.at[ph, pl.ds(0, C - 1)], ar_send.at[ph, 0])
        wait_for(ar2.at[ph, pl.ds(0, R - 1)], ar_send.at[ph, 1])
        wait_for(ar1.at[ph, pl.ds(0, C - 1)], ar_send.at[ph, 2])

    am_root = col == col_to
    other_root = other == col_to
    OTHERS = (1, -1, 2)

    def other_is_root(off):
        return (mod4(y + off) == y_to) & (core == core_to)

    def first_sends(ph):
        here = rows.at[ph, col]
        @pl.when(jnp.logical_not(am_root))
        def _():
            remote(here, here, ysend.at[ph, 0], yrecv.at[ph, col], (row, col_to)).start()
        for peer, flag in helpers_to:
            copy = remote(here, cols.at[ph, x // 2, col], lsend.at[ph], precv.at[ph, x // 2, col], peer)
            when(flag, copy.start)

    def line_start(ph):
        here = rows.at[ph, col]
        for n, off in enumerate(OTHERS):
            @pl.when(jnp.logical_not(other_is_root(off)))
            def _():
                remote(here, here, ysend.at[ph, 1 + n], yrecv.at[ph, col], at_y(off)).start()
        @pl.when(jnp.logical_not(other_root))
        def _():
            remote(here, here, ysend.at[ph, 4], yrecv.at[ph, col], (row, other)).start()

    def line_step(ph, kk):
        k = natural(kk)
        here = rows.at[ph, k]
        @pl.when(jnp.logical_not(am_root))
        def _():
            wait_for(here, yrecv.at[ph, k])
        if kk % 2 == 0:
            @pl.when(jnp.logical_not(other_root))
            def _():
                remote(here, here, ysend.at[ph, 4 + kk // 2], yrecv.at[ph, k], (row, other)).start()

    def plane_step(ph, kk):
        k = natural(kk)
        for s in range(2):
            here = cols.at[ph, s, k]

            def send(source):
                for peer, flag in next_chips(kk, s):
                    when(flag, remote(source, here, psend.at[ph, s, kk], precv.at[ph, s, k], peer).start)

            @pl.when(roots[s])
            def _():
                if kk:
                    wait_for(rows.at[ph, k], yrecv.at[ph, k])
                send(rows.at[ph, k])

            @pl.when(helper(kk, s))
            def _():
                wait_for(here, precv.at[ph, s, k])
                send(here)

    ORDER = (0, 1, 2, 4, 3, 5, 6, 7)

    def gather(ph, extra):
        first_sends(ph)
        for tick, kk in enumerate(ORDER):
            plane_step(ph, kk)
            if tick == 4:
                line_start(ph)
            extra(tick)

    def gather_wait(ph):
        for s in range(2):
            for kk in range(8):
                k = natural(kk)
                @pl.when(jnp.logical_not(helper(kk, s) | roots[s]))
                def _():
                    wait_for(cols.at[ph, s, k], precv.at[ph, s, k])
            @pl.when(roots[s])
            def _():
                cols[ph, s] = rows[ph]

    def gather_finish(ph):
        sent = [jnp.logical_not(am_root)] + [jnp.logical_not(other_is_root(off)) for off in OTHERS]
        for n, flag in enumerate(sent + [jnp.logical_not(other_root)] * 4):
            @pl.when(flag)
            def _():
                wait_for(rows.at[ph, 0], ysend.at[ph, n])
        for count in sorted(set(counts)):
            @pl.when(count_to == count)
            def _():
                wait_for(cols.at[ph, 0, pl.ds(0, count)], lsend.at[ph])
        for kk in range(8):
            heads, groups = PATTERNS[kk]
            sizes = sorted(set(len(group) for group in groups) - {0})
            for s in range(2):
                for size in sizes:
                    keys = [head for head, group in zip(heads, groups) if len(group) == size]
                    @pl.when(among(codes[s], keys))
                    def _():
                        wait_for(cols.at[ph, 0, pl.ds(0, size)], psend.at[ph, s, kk])

    def split_h(i):
        h_copies[i].wait()
        hi, lo = halves(h_out[pl.ds(i * h_rows, h_rows)])
        hhi[pl.ds(i * h_rows, h_rows)] = hi
        hlo[pl.ds(i * h_rows, h_rows)] = lo

    def first_extra(tick):
        if tick == 0:
            part[0] = dot6(rows[0, col], rows[0, col], TN)
        if tick == 4:
            reduce_step(0, 0)
        split_h(tick)

    gather(0, first_extra)
    reduce_step(0, 1)
    gather_wait(0)

    def block_rows(ph, s, b):
        flat = cols.at[ph, s].reshape(local_rows, B)
        return flat[pl.ds(b * B, B)]

    for b in range(blocks):
        for s in range(2):
            at = pl.ds((2 * b + s) * B, B)
            hi, lo = halves(block_rows(0, s, b))
            vw[at, :B] = hi
            vw[at, B:] = lo
            zhi[at, :B] = hi
            zlo[at, :B] = lo

    order = (2, 1, -1, 0)
    two_rows = 2 * piece
    v_rows = rows.at[0].reshape(local_rows, B)
    p_rows = rows.at[1].reshape(local_rows, B)

    def part_of(j, which):
        start = mod4(y + order[j]) * two_rows + which * piece
        return pl.ds(pl.multiple_of(start, 16), piece)

    def sum_pair(j):
        wait_for(sib_in.at[j], sib_recv.at[j])
        ring_out[j] = acc[part_of(j, core)] + sib_in[j]
        if order[j]:
            remote(ring_out.at[j], ring_in.at[j], ring_send.at[j], ring_recv.at[j], at_y(order[j])).start()

    for j, off in enumerate(order):
        take = pl.ds(pl.multiple_of(mod4(y + off) * two_rows, 32), two_rows)
        both = dot1(hhi[take], vw[...]) + dot1(hlo[take], vw[...])
        acc[take] = both[:, :B] + both[:, B:]
        remote(
            acc.at[part_of(j, 1 - core)], sib_in.at[j], sib_send.at[j], sib_recv.at[j], (row, other)
        ).start()
        if j:
            sum_pair(j - 1)
    sum_pair(3)
    for kk in ORDER[1:]:
        line_step(0, kk)
    part[1] = dot6(v_rows[...], acc[...], TN)
    reduce_step(1, 0)
    reduce_step(0, 2)
    p_piece = ring_out[3]
    for j in range(3):
        wait_for(ring_in.at[j], ring_recv.at[j])
        p_piece = p_piece + ring_in[j]
    rows[1, col] = p_piece

    eye_r = lax.broadcasted_iota(jnp.int32, (B, B), 0)
    eye_c = lax.broadcasted_iota(jnp.int32, (B, B), 1)
    gram = arout.at[0]

    def inverse_step(i):
        if i == 0:
            g = gram[...]
            half = jnp.sum(jnp.where(eye_r == eye_c, g, 0.0), axis=1, keepdims=True) * 0.5
            start = -(jnp.where(eye_c > eye_r, g, 0.0) / half)
            inverse[...] = start + jnp.where(eye_r == eye_c, 1.0, 0.0)
            power[...] = dot6(start, start)
        elif i < 7:
            now = power[...]
            inverse[...] = inverse[...] + dot6(inverse[...], now)
            if i < 6:
                power[...] = dot6(now, now)
        else:
            g = gram[...]
            half = jnp.sum(jnp.where(eye_r == eye_c, g, 0.0), axis=0, keepdims=True) * 0.5
            inverse[...] = inverse[...] / half

    def second_extra(tick):
        if tick == 0:
            reduce_step(1, 1)
            reduce_step(0, 3)
        inverse_step(tick)

    gather(1, second_extra)
    reduce_step(1, 2)
    for kk in ORDER[1:]:
        line_step(1, kk)
    reduce_step(1, 3)

    u = inverse[...]
    middle = dot6(dot6(u, arout[1], TN), u)
    middle = -0.5 * (middle + middle.T)
    chunk = 384
    for t in range(local_rows // chunk):
        at = pl.ds(t * chunk, chunk)
        v, p = v_rows[at], p_rows[at]
        hi, lo = halves(dot6(p, u) + dot6(v, middle))
        whi[at, :B] = hi
        wlo[at, :B] = lo
        hi, lo = halves(dot6(v, u, NT))
        whi[at, B:] = hi
        wlo[at, B:] = lo

    gather_wait(1)
    for b in range(blocks):
        for s in range(2):
            at = pl.ds((2 * b + s) * B, B)
            hi, lo = halves(block_rows(1, s, b))
            zhi[at, B:] = hi
            zlo[at, B:] = lo

    for ph in range(2):
        gather_finish(ph)
        reduce_finish(ph)
    for j in range(4):
        wait_for(sib_in.at[j], sib_send.at[j])
    for j in range(3):
        wait_for(ring_in.at[j], ring_send.at[j])


def update_kernel(h_ref, whi, wlo, zhi, zlo, out_ref, tiles, sem):
    width = tiles.shape[2]
    slots = tiles.shape[0]
    steps = h_ref.shape[1] // width

    def copy(b):
        slot = lax.rem(b, slots)
        return pltpu.make_async_copy(
            tiles.at[slot], out_ref.at[:, pl.ds(pl.multiple_of(b * width, width), width)], sem.at[slot]
        )

    def step(b, carry):
        @pl.when(b >= slots)
        def _():
            copy(b - slots).wait()

        at = pl.ds(pl.multiple_of(b * width, width), width)
        high = zhi[at]
        change = dot1(whi[...], high, NT) + dot1(wlo[...], high, NT) + dot1(whi[...], zlo[at], NT)
        tiles[lax.rem(b, slots)] = h_ref[:, at] - change
        copy(b).start()
        return carry

    lax.fori_loop(0, steps, step, 0)
    for b in range(steps - slots, steps):
        copy(b).wait()


def body(hamiltonian, panel):
    m, n = hamiltonian.shape
    piece = panel.shape[0]
    vmem = pl.BlockSpec(memory_space=pltpu.VMEM)
    hbm = pl.BlockSpec(memory_space=pl.ANY)
    dma = pltpu.SemaphoreType.DMA
    operands = pl.pallas_call(
        panel_kernel,
        out_shape=[
            jax.ShapeDtypeStruct((m, n), F32),
            jax.ShapeDtypeStruct((m, 2 * B), BF16),
            jax.ShapeDtypeStruct((m, 2 * B), BF16),
            jax.ShapeDtypeStruct((n, 2 * B), BF16),
            jax.ShapeDtypeStruct((n, 2 * B), BF16),
        ],
        in_specs=[hbm, hbm],
        out_specs=[vmem] * 5,
        scratch_shapes=[
            pltpu.VMEM((m, n), BF16),
            pltpu.VMEM((m, n), BF16),
            pltpu.VMEM((n, 2 * B), BF16),
            pltpu.VMEM((2, C, piece, B), F32),
            pltpu.VMEM((2, 2, C, piece, B), F32),
            pltpu.VMEM((m, B), F32),
            pltpu.VMEM((4, piece, B), F32),
            pltpu.VMEM((3, piece, B), F32),
            pltpu.VMEM((4, piece, B), F32),
            pltpu.VMEM((piece, B), F32),
            pltpu.VMEM((2, B, B), F32),
            pltpu.VMEM((2, C, 16, B), F32),
            pltpu.VMEM((2, R, 16, B), F32),
            pltpu.VMEM((2, B, B), F32),
            pltpu.VMEM((B, B), F32),
            pltpu.VMEM((B, B), F32),
            dma,
            dma((8,)),
            dma((2, 8)),
            dma((2, C)),
            dma((2,)),
            dma((2, 2, C)),
            dma((2, 2, C)),
            dma((4,)),
            dma((4,)),
            dma((3,)),
            dma((3,)),
            dma((2, 3)),
            dma((2, 3)),
        ],
        compiler_params=pltpu.CompilerParams(
            collective_id=0, has_side_effects=True, vmem_limit_bytes=40 * 2**20
        ),
        cost_estimate=pl.CostEstimate(flops=8 * m * n * B, bytes_accessed=4 * m * n, transcendentals=0),
        name="panel_products",
    )(hamiltonian, panel)
    return pl.pallas_call(
        update_kernel,
        out_shape=jax.ShapeDtypeStruct((m, n), F32),
        in_specs=[vmem] * 5,
        out_specs=hbm,
        scratch_shapes=[pltpu.VMEM((3, m, 2 * B), F32), dma((3,))],
        compiler_params=pltpu.CompilerParams(vmem_limit_bytes=24 * 2**20),
        cost_estimate=pl.CostEstimate(flops=12 * m * n * B, bytes_accessed=4 * m * n, transcendentals=0),
        name="rank_update",
    )(*operands)


def solution(mesh):
    return jax.shard_map(
        body,
        mesh=mesh,
        in_specs=(P("row", "col"), P(("row", "col"), None)),
        out_specs=P("row", "col"),
        check_vma=False,
    )
```

```python
import jax
import jax.numpy as jnp
from jax import lax
from jax.experimental import pallas as pl
from jax.experimental.pallas import tpu as pltpu
from jax.sharding import PartitionSpec as P

B = 128
R = 16
C = 8
MESH = pl.DeviceIdType.MESH
F32 = jnp.float32
BF16 = jnp.bfloat16
HIGHEST = lax.Precision.HIGHEST

PATTERNS = (
    ((0, 2, 4, 8, 11, 12, 13), ((), (1, 3, 6, 14), (5, 7), (), (10, 15), (), (9,))),
    ((0, 1, 4, 7, 8, 11, 12, 15), ((), (2, 13), (5,), (3, 6), (9,), (10,), (), (14,))),
    ((0, 2, 4, 11, 13), ((3,), (1, 6, 14), (5,), (7, 8, 10, 15), (9, 12))),
    ((0, 5, 7, 8, 14), ((1,), (9,), (3, 4, 6, 11), (12,), (2, 10, 13, 15))),
    ((0, 2, 4, 9, 12), ((), (1, 3, 6, 14), (5, 7, 8), (10, 11, 13), (15,))),
    ((0, 5, 7, 8, 14), ((3,), (1, 9), (4, 6), (11, 12), (2, 10, 13, 15))),
    ((0, 5, 7, 14), ((8, 12), (1, 6, 9, 13), (3, 4, 11), (2, 10, 15))),
    ((0, 9, 10, 15), ((1, 4, 12), (5, 8, 13), (2, 6, 11, 14), (3, 7))),
)
NN = (((1,), (0,)), ((), ()))
NT = (((1,), (1,)), ((), ()))
TN = (((0,), (0,)), ((), ()))


def dot6(a, b, dims=NN):
    return lax.dot_general(a, b, dims, precision=HIGHEST, preferred_element_type=F32)


def dot1(a, b, dims=NN):
    return lax.dot_general(a, b, dims, preferred_element_type=F32)


def halves(v):
    hi = v.astype(BF16)
    return hi, (v - hi.astype(F32)).astype(BF16)


def mod4(v):
    return lax.rem(v + 8, 4)


def panel_kernel(
    h_ref, panel_ref, h_out, whi, wlo, zhi, zlo,
    hhi, hlo, vw, rows, cols, acc, sib_in, ring_in, ring_out, raw_panel,
    part, ar1, ar2, ar3, arout, power, inverse,
    p_sem, h_sem, ysend, yrecv, lsend, psend, precv, sib_send, sib_recv, ring_send, ring_recv, ar_send, ar_recv,
):
    row = lax.axis_index("row")
    col = lax.axis_index("col")
    x, z = row // 4, lax.rem(row, 4)
    y, core = col // 2, lax.rem(col, 2)
    other = col + 1 - 2 * core
    panel_copy = pltpu.make_async_copy(panel_ref, raw_panel, p_sem)
    panel_copy.start()
    piece = panel_ref.shape[0]
    local_rows = h_out.shape[0]
    blocks = local_rows // B

    def at_y(off):
        return (row, mod4(y + off) * 2 + core)

    line_peers = [(row, lax.rem(col + o, C)) for o in range(1, C)]
    x_peers = [(mod4(x + o) * 4 + z, col) for o in range(1, 4)]
    z_peers = [(x * 4 + mod4(z + o), col) for o in range(1, 4)]
    plane_peers = [(lax.rem(row + o, R), col) for o in range(1, R)]

    sz = 1 - 2 * core
    sx = 1 - 2 * (y // 2)
    z0 = 2 * lax.rem(y, 2) + core
    x0s = [y // 2, y // 2 + 2]
    codes = [4 * mod4((x - x0) * sx) + mod4((z - z0) * sz) for x0 in x0s]
    roots = [code == 0 for code in codes]
    OFFS = (0, -1, 1, 2)

    def natural(kk):
        return mod4(y + OFFS[kk // 2]) * 2 + (core if kk % 2 == 0 else 1 - core)

    def chain(key, keys, values):
        out = values[0]
        for k, v in zip(keys[1:], values[1:]):
            out = jnp.where(key == k, v, out)
        return out

    def among(key, keys):
        found = key == keys[0]
        for k in keys[1:]:
            found = found | (key == k)
        return found

    def helper(kk, s):
        return among(codes[s], PATTERNS[kk][0][1:])

    def next_chips(kk, s):
        heads, groups = PATTERNS[kk]
        for n in range(max(len(group) for group in groups)):
            pairs = [(head, group[n]) for head, group in zip(heads, groups) if len(group) > n]
            keys = [head for head, _ in pairs]
            steps = [4 * ((to // 4 - head // 4) % 4) + (to % 4 - head % 4) % 4 for head, to in pairs]
            step = chain(codes[s], keys, steps)
            peer = (mod4(x + sx * (step // 4)) * 4 + mod4(z + sz * lax.rem(step, 4)), col)
            yield peer, None if len(keys) == len(heads) else among(codes[s], keys)

    def when(flag, act):
        if flag is None:
            act()
        else:
            pl.when(flag)(act)

    y_to = lax.rem(row, C) // 2
    core_to = lax.rem(z, 2)
    col_to = y_to * 2 + core_to
    off_to = mod4(y - y_to)
    index_to = jnp.where(off_to == 0, 0, jnp.where(off_to == 3, 1, jnp.where(off_to == 1, 2, 3)))
    kk_to = 2 * index_to + jnp.where(core == core_to, 0, 1)
    sx_to = 1 - 2 * (y_to // 2)
    sz_to = 1 - 2 * core_to
    counts = [len(heads) - 1 for heads, _ in PATTERNS]
    count_to = chain(kk_to, range(8), counts)
    helpers_to = []
    for n in range(max(counts)):
        having = [kk for kk in range(8) if counts[kk] > n]
        step = chain(kk_to, having, [PATTERNS[kk][0][n + 1] for kk in having])
        peer = (mod4(x + sx_to * (step // 4)) * 4 + mod4(z + sz_to * lax.rem(step, 4)), col_to)
        helpers_to.append((peer, None if len(having) == 8 else count_to > n))

    barrier = pltpu.get_barrier_semaphore()
    for peer in line_peers + plane_peers:
        pl.semaphore_signal(barrier, inc=1, device_id=peer, device_id_type=MESH)
    for kk in range(8):
        for s in range(2):
            @pl.when(helper(kk, s))
            def _():
                pl.semaphore_signal(
                    barrier, inc=1, device_id=(x0s[s] * 4 + z0, natural(kk)), device_id_type=MESH
                )

    n_h = h_sem.shape[0]
    h_rows = local_rows // n_h
    h_copies = [
        pltpu.make_async_copy(
            h_ref.at[pl.ds(i * h_rows, h_rows)], h_out.at[pl.ds(i * h_rows, h_rows)], h_sem.at[i]
        )
        for i in range(n_h)
    ]
    for copy in h_copies:
        copy.start()

    position = col * piece + lax.broadcasted_iota(jnp.int32, (piece, B), 0)
    column = lax.broadcasted_iota(jnp.int32, (piece, B), 1)
    global_block = (position >> 7) * R + row
    within = position & (B - 1)
    panel_copy.wait()
    raw = raw_panel[...]
    unit = jnp.where(column < within, raw, jnp.where(column == within, 1.0, 0.0))
    kept = jnp.where(global_block == 1, unit, 0.0)
    rows[0, col] = jnp.where(global_block >= 2, raw, kept)

    pl.semaphore_wait(barrier, len(line_peers) + len(plane_peers) + count_to)

    def remote(src, dst, send, recv, peer):
        return pltpu.make_async_remote_copy(
            src_ref=src, dst_ref=dst, send_sem=send, recv_sem=recv, device_id=peer, device_id_type=MESH
        )

    def wait_for(ref, sem):
        pltpu.make_async_copy(ref, ref, sem).wait()

    mine16 = pl.ds(pl.multiple_of(col * 16, 16), 16)

    def reduce_step(ph, step):
        if step == 0:
            for peer in line_peers:
                remote(
                    part.at[ph, pl.ds(pl.multiple_of(peer[1] * 16, 16), 16)], ar1.at[ph, col],
                    ar_send.at[ph, 0], ar_recv.at[ph, 0], peer,
                ).start()
            ar1[ph, col] = part[ph, mine16]
        elif step == 1:
            wait_for(ar1.at[ph, pl.ds(0, C - 1)], ar_recv.at[ph, 0])
            ar2[ph, x] = sum(ar1[ph, i] for i in range(C))
            for peer in x_peers:
                remote(ar2.at[ph, x], ar2.at[ph, x], ar_send.at[ph, 1], ar_recv.at[ph, 1], peer).start()
        elif step == 2:
            wait_for(ar2.at[ph, pl.ds(0, 3)], ar_recv.at[ph, 1])
            ar3[ph, z] = sum(ar2[ph, i] for i in range(4))
            for peer in z_peers:
                remote(ar3.at[ph, z], ar3.at[ph, z], ar_send.at[ph, 2], ar_recv.at[ph, 2], peer).start()
        elif step == 3:
            wait_for(ar3.at[ph, pl.ds(0, 3)], ar_recv.at[ph, 2])
            arout[ph, mine16] = sum(ar3[ph, i] for i in range(4))
            for peer in line_peers:
                remote(arout.at[ph, mine16], arout.at[ph, mine16], ar_send.at[ph, 3], ar_recv.at[ph, 3], peer).start()
        else:
            wait_for(arout.at[ph, pl.ds(0, 16 * (C - 1))], ar_recv.at[ph, 3])

    def reduce_finish(ph):
        for step, count in enumerate((C - 1, 3, 3, C - 1)):
            wait_for(ar1.at[ph, pl.ds(0, count)], ar_send.at[ph, step])

    am_root = col == col_to
    other_root = other == col_to
    OTHERS = (1, -1, 2)

    def other_is_root(off):
        return (mod4(y + off) == y_to) & (core == core_to)

    def first_sends(ph):
        here = rows.at[ph, col]
        @pl.when(jnp.logical_not(am_root))
        def _():
            remote(here, here, ysend.at[ph, 0], yrecv.at[ph, col], (row, col_to)).start()
        for peer, flag in helpers_to:
            copy = remote(here, cols.at[ph, x // 2, col], lsend.at[ph], precv.at[ph, x // 2, col], peer)
            when(flag, copy.start)

    def line_start(ph):
        here = rows.at[ph, col]
        for n, off in enumerate(OTHERS):
            @pl.when(jnp.logical_not(other_is_root(off)))
            def _():
                remote(here, here, ysend.at[ph, 1 + n], yrecv.at[ph, col], at_y(off)).start()
        @pl.when(jnp.logical_not(other_root))
        def _():
            remote(here, here, ysend.at[ph, 4], yrecv.at[ph, col], (row, other)).start()

    def line_step(ph, kk):
        k = natural(kk)
        here = rows.at[ph, k]
        @pl.when(jnp.logical_not(am_root))
        def _():
            wait_for(here, yrecv.at[ph, k])
        if kk % 2 == 0:
            @pl.when(jnp.logical_not(other_root))
            def _():
                remote(here, here, ysend.at[ph, 4 + kk // 2], yrecv.at[ph, k], (row, other)).start()

    def plane_step(ph, kk):
        k = natural(kk)
        for s in range(2):
            here = cols.at[ph, s, k]

            def send(source):
                for peer, flag in next_chips(kk, s):
                    when(flag, remote(source, here, psend.at[ph, s, kk], precv.at[ph, s, k], peer).start)

            @pl.when(roots[s])
            def _():
                if kk:
                    wait_for(rows.at[ph, k], yrecv.at[ph, k])
                send(rows.at[ph, k])

            @pl.when(helper(kk, s))
            def _():
                wait_for(here, precv.at[ph, s, k])
                send(here)

    ORDER = (0, 1, 2, 4, 3, 5, 6, 7)

    def gather(ph, extra):
        first_sends(ph)
        for tick, kk in enumerate(ORDER):
            plane_step(ph, kk)
            if tick == 4:
                line_start(ph)
            extra(tick)

    def gather_wait(ph):
        for s in range(2):
            for kk in range(8):
                k = natural(kk)
                @pl.when(jnp.logical_not(helper(kk, s) | roots[s]))
                def _():
                    wait_for(cols.at[ph, s, k], precv.at[ph, s, k])
            @pl.when(roots[s])
            def _():
                cols[ph, s] = rows[ph]

    def gather_finish(ph):
        sent = [jnp.logical_not(am_root)] + [jnp.logical_not(other_is_root(off)) for off in OTHERS]
        for n, flag in enumerate(sent + [jnp.logical_not(other_root)] * 4):
            @pl.when(flag)
            def _():
                wait_for(rows.at[ph, 0], ysend.at[ph, n])
        for count in sorted(set(counts)):
            @pl.when(count_to == count)
            def _():
                wait_for(cols.at[ph, 0, pl.ds(0, count)], lsend.at[ph])
        for kk in range(8):
            heads, groups = PATTERNS[kk]
            sizes = sorted(set(len(group) for group in groups) - {0})
            for s in range(2):
                for size in sizes:
                    keys = [head for head, group in zip(heads, groups) if len(group) == size]
                    @pl.when(among(codes[s], keys))
                    def _():
                        wait_for(cols.at[ph, 0, pl.ds(0, size)], psend.at[ph, s, kk])

    def split_h(i):
        h_copies[i].wait()
        hi, lo = halves(h_out[pl.ds(i * h_rows, h_rows)])
        hhi[pl.ds(i * h_rows, h_rows)] = hi
        hlo[pl.ds(i * h_rows, h_rows)] = lo

    def first_extra(tick):
        if tick == 0:
            part[0] = dot6(rows[0, col], rows[0, col], TN)
        if tick == 4:
            reduce_step(0, 0)

    gather(0, first_extra)
    for i in range(n_h):
        split_h(i)
        if i == 3:
            reduce_step(0, 1)
    reduce_step(0, 2)
    gather_wait(0)

    def block_rows(ph, s, b):
        flat = cols.at[ph, s].reshape(local_rows, B)
        return flat[pl.ds(b * B, B)]

    for b in range(blocks):
        for s in range(2):
            at = pl.ds((2 * b + s) * B, B)
            hi, lo = halves(block_rows(0, s, b))
            vw[at, :B] = hi
            vw[at, B:] = lo
            zhi[at, :B] = hi
            zlo[at, :B] = lo

    order = (2, 1, -1, 0)
    two_rows = 2 * piece
    v_rows = rows.at[0].reshape(local_rows, B)
    p_rows = rows.at[1].reshape(local_rows, B)

    def part_of(j, which):
        start = mod4(y + order[j]) * two_rows + which * piece
        return pl.ds(pl.multiple_of(start, 16), piece)

    def sum_pair(j):
        wait_for(sib_in.at[j], sib_recv.at[j])
        ring_out[j] = acc[part_of(j, core)] + sib_in[j]
        if order[j]:
            remote(ring_out.at[j], ring_in.at[j], ring_send.at[j], ring_recv.at[j], at_y(order[j])).start()

    for j, off in enumerate(order):
        take = pl.ds(pl.multiple_of(mod4(y + off) * two_rows, 32), two_rows)
        both = dot1(hhi[take], vw[...]) + dot1(hlo[take], vw[...])
        acc[take] = both[:, :B] + both[:, B:]
        remote(
            acc.at[part_of(j, 1 - core)], sib_in.at[j], sib_send.at[j], sib_recv.at[j], (row, other)
        ).start()
        if j:
            sum_pair(j - 1)
    sum_pair(3)
    for kk in ORDER[1:]:
        line_step(0, kk)
    part[1] = dot6(v_rows[...], acc[...], TN)
    reduce_step(1, 0)
    reduce_step(0, 3)
    p_piece = ring_out[3]
    for j in range(3):
        wait_for(ring_in.at[j], ring_recv.at[j])
        p_piece = p_piece + ring_in[j]
    rows[1, col] = p_piece

    eye_r = lax.broadcasted_iota(jnp.int32, (B, B), 0)
    eye_c = lax.broadcasted_iota(jnp.int32, (B, B), 1)
    gram = arout.at[0]

    def inverse_step(i):
        if i == 0:
            g = gram[...]
            half = jnp.sum(jnp.where(eye_r == eye_c, g, 0.0), axis=1, keepdims=True) * 0.5
            start = -(jnp.where(eye_c > eye_r, g, 0.0) / half)
            inverse[...] = start + jnp.where(eye_r == eye_c, 1.0, 0.0)
            power[...] = dot6(start, start)
        elif i < 7:
            now = power[...]
            inverse[...] = inverse[...] + dot6(inverse[...], now)
            if i < 6:
                power[...] = dot6(now, now)
        else:
            g = gram[...]
            half = jnp.sum(jnp.where(eye_r == eye_c, g, 0.0), axis=0, keepdims=True) * 0.5
            inverse[...] = inverse[...] / half

    def second_extra(tick):
        if tick == 0:
            reduce_step(1, 1)
        if tick == 5:
            reduce_step(1, 2)

    gather(1, second_extra)
    reduce_step(1, 3)
    reduce_step(0, 4)
    for i in range(8):
        inverse_step(i)
    for kk in ORDER[1:]:
        line_step(1, kk)
    reduce_step(1, 4)

    u = inverse[...]
    middle = dot6(dot6(u, arout[1], TN), u)
    middle = -0.5 * (middle + middle.T)
    chunk = 384
    for t in range(local_rows // chunk):
        at = pl.ds(t * chunk, chunk)
        v, p = v_rows[at], p_rows[at]
        hi, lo = halves(dot6(p, u) + dot6(v, middle))
        whi[at, :B] = hi
        wlo[at, :B] = lo
        hi, lo = halves(dot6(v, u, NT))
        whi[at, B:] = hi
        wlo[at, B:] = lo

    gather_wait(1)
    for b in range(blocks):
        for s in range(2):
            at = pl.ds((2 * b + s) * B, B)
            hi, lo = halves(block_rows(1, s, b))
            zhi[at, B:] = hi
            zlo[at, B:] = lo

    for ph in range(2):
        gather_finish(ph)
        reduce_finish(ph)
    for j in range(4):
        wait_for(sib_in.at[j], sib_send.at[j])
    for j in range(3):
        wait_for(ring_in.at[j], ring_send.at[j])


def update_kernel(h_ref, whi, wlo, zhi, zlo, out_ref, tiles, sem):
    width = tiles.shape[2]
    slots = tiles.shape[0]
    steps = h_ref.shape[1] // width
    height = 288

    def copy(b):
        slot = lax.rem(b, slots)
        return pltpu.make_async_copy(
            tiles.at[slot], out_ref.at[:, pl.ds(pl.multiple_of(b * width, width), width)], sem.at[slot]
        )

    def step(b, carry):
        @pl.when(b >= slots)
        def _():
            copy(b - slots).wait()

        at = pl.ds(pl.multiple_of(b * width, width), width)
        high, low = zhi[at], zlo[at]
        for start in range(0, h_ref.shape[0], height):
            take = pl.ds(start, height)
            w = whi[take]
            change = dot1(w, high, NT) + dot1(wlo[take], high, NT) + dot1(w, low, NT)
            tiles[lax.rem(b, slots), take] = h_ref[take, at] - change
        copy(b).start()
        return carry

    lax.fori_loop(0, steps, step, 0)
    for b in range(steps - slots, steps):
        copy(b).wait()


def body(hamiltonian, panel):
    m, n = hamiltonian.shape
    piece = panel.shape[0]
    vmem = pl.BlockSpec(memory_space=pltpu.VMEM)
    hbm = pl.BlockSpec(memory_space=pl.ANY)
    dma = pltpu.SemaphoreType.DMA
    operands = pl.pallas_call(
        panel_kernel,
        out_shape=[
            jax.ShapeDtypeStruct((m, n), F32),
            jax.ShapeDtypeStruct((m, 2 * B), BF16),
            jax.ShapeDtypeStruct((m, 2 * B), BF16),
            jax.ShapeDtypeStruct((n, 2 * B), BF16),
            jax.ShapeDtypeStruct((n, 2 * B), BF16),
        ],
        in_specs=[hbm, hbm],
        out_specs=[vmem] * 5,
        scratch_shapes=[
            pltpu.VMEM((m, n), BF16),
            pltpu.VMEM((m, n), BF16),
            pltpu.VMEM((n, 2 * B), BF16),
            pltpu.VMEM((2, C, piece, B), F32),
            pltpu.VMEM((2, 2, C, piece, B), F32),
            pltpu.VMEM((m, B), F32),
            pltpu.VMEM((4, piece, B), F32),
            pltpu.VMEM((3, piece, B), F32),
            pltpu.VMEM((4, piece, B), F32),
            pltpu.VMEM((piece, B), F32),
            pltpu.VMEM((2, B, B), F32),
            pltpu.VMEM((2, C, 16, B), F32),
            pltpu.VMEM((2, 4, 16, B), F32),
            pltpu.VMEM((2, 4, 16, B), F32),
            pltpu.VMEM((2, B, B), F32),
            pltpu.VMEM((B, B), F32),
            pltpu.VMEM((B, B), F32),
            dma,
            dma((8,)),
            dma((2, 8)),
            dma((2, C)),
            dma((2,)),
            dma((2, 2, C)),
            dma((2, 2, C)),
            dma((4,)),
            dma((4,)),
            dma((3,)),
            dma((3,)),
            dma((2, 4)),
            dma((2, 4)),
        ],
        compiler_params=pltpu.CompilerParams(
            collective_id=0, has_side_effects=True, vmem_limit_bytes=40 * 2**20
        ),
        cost_estimate=pl.CostEstimate(flops=8 * m * n * B, bytes_accessed=4 * m * n, transcendentals=0),
        name="panel_products",
    )(hamiltonian, panel)
    return pl.pallas_call(
        update_kernel,
        out_shape=jax.ShapeDtypeStruct((m, n), F32),
        in_specs=[vmem] * 5,
        out_specs=hbm,
        scratch_shapes=[pltpu.VMEM((2, m, 6 * B), F32), dma((2,))],
        compiler_params=pltpu.CompilerParams(vmem_limit_bytes=24 * 2**20),
        cost_estimate=pl.CostEstimate(flops=12 * m * n * B, bytes_accessed=4 * m * n, transcendentals=0),
        name="rank_update",
    )(*operands)


def solution(mesh):
    return jax.shard_map(
        body,
        mesh=mesh,
        in_specs=(P("row", "col"), P(("row", "col"), None)),
        out_specs=P("row", "col"),
        check_vma=False,
    )
```

```python
import jax
import jax.numpy as jnp
from jax import lax
from jax.experimental import pallas as pl
from jax.experimental.pallas import tpu as pltpu
from jax.sharding import PartitionSpec as P

B = 128
R = 16
C = 8
MESH = pl.DeviceIdType.MESH
F32 = jnp.float32
BF16 = jnp.bfloat16
HIGHEST = lax.Precision.HIGHEST

PATTERNS = (
    ((0, 2, 4, 8, 11, 12, 13), ((), (1, 3, 6, 14), (5, 7), (), (10, 15), (), (9,))),
    ((0, 1, 4, 7, 8, 11, 12, 15), ((), (2, 13), (5,), (3, 6), (9,), (10,), (), (14,))),
    ((0, 2, 4, 11, 13), ((3,), (1, 6, 14), (5,), (7, 8, 10, 15), (9, 12))),
    ((0, 5, 7, 8, 14), ((1,), (9,), (3, 4, 6, 11), (12,), (2, 10, 13, 15))),
    ((0, 2, 4, 9, 12), ((), (1, 3, 6, 14), (5, 7, 8), (10, 11, 13), (15,))),
    ((0, 5, 7, 8, 14), ((3,), (1, 9), (4, 6), (11, 12), (2, 10, 13, 15))),
    ((0, 5, 7, 14), ((8, 12), (1, 6, 9, 13), (3, 4, 11), (2, 10, 15))),
    ((0, 9, 10, 15), ((1, 4, 12), (5, 8, 13), (2, 6, 11, 14), (3, 7))),
)
NN = (((1,), (0,)), ((), ()))
NT = (((1,), (1,)), ((), ()))
TN = (((0,), (0,)), ((), ()))


def dot6(a, b, dims=NN):
    return lax.dot_general(a, b, dims, precision=HIGHEST, preferred_element_type=F32)


def dot1(a, b, dims=NN):
    return lax.dot_general(a, b, dims, preferred_element_type=F32)


def halves(v):
    hi = v.astype(BF16)
    return hi, (v - hi.astype(F32)).astype(BF16)


def mod4(v):
    return lax.rem(v + 8, 4)


def panel_kernel(
    h_ref, panel_ref, h_out, whi, wlo, zhi, zlo,
    hhi, hlo, vw, rows, cols, acc, sib_in, ring_in, ring_out, raw_panel,
    part, ar1, ar2, arout, power, inverse,
    p_sem, h_sem, ysend, yrecv, lsend, psend, precv, sib_send, sib_recv, ring_send, ring_recv, ar_send, ar_recv,
):
    row = lax.axis_index("row")
    col = lax.axis_index("col")
    x, z = row // 4, lax.rem(row, 4)
    y, core = col // 2, lax.rem(col, 2)
    other = col + 1 - 2 * core
    panel_copy = pltpu.make_async_copy(panel_ref, raw_panel, p_sem)
    panel_copy.start()
    piece = panel_ref.shape[0]
    local_rows = h_out.shape[0]
    blocks = local_rows // B

    def at_y(off):
        return (row, mod4(y + off) * 2 + core)

    line_peers = [(row, lax.rem(col + o, C)) for o in range(1, C)]
    plane_peers = [(lax.rem(row + o, R), col) for o in range(1, R)]

    sz = 1 - 2 * core
    sx = 1 - 2 * (y // 2)
    z0 = 2 * lax.rem(y, 2) + core
    x0s = [y // 2, y // 2 + 2]
    codes = [4 * mod4((x - x0) * sx) + mod4((z - z0) * sz) for x0 in x0s]
    roots = [code == 0 for code in codes]
    OFFS = (0, -1, 1, 2)

    def natural(kk):
        return mod4(y + OFFS[kk // 2]) * 2 + (core if kk % 2 == 0 else 1 - core)

    def chain(key, keys, values):
        out = values[0]
        for k, v in zip(keys[1:], values[1:]):
            out = jnp.where(key == k, v, out)
        return out

    def among(key, keys):
        found = key == keys[0]
        for k in keys[1:]:
            found = found | (key == k)
        return found

    def helper(kk, s):
        return among(codes[s], PATTERNS[kk][0][1:])

    def next_chips(kk, s):
        heads, groups = PATTERNS[kk]
        for n in range(max(len(group) for group in groups)):
            pairs = [(head, group[n]) for head, group in zip(heads, groups) if len(group) > n]
            keys = [head for head, _ in pairs]
            steps = [4 * ((to // 4 - head // 4) % 4) + (to % 4 - head % 4) % 4 for head, to in pairs]
            step = chain(codes[s], keys, steps)
            peer = (mod4(x + sx * (step // 4)) * 4 + mod4(z + sz * lax.rem(step, 4)), col)
            yield peer, None if len(keys) == len(heads) else among(codes[s], keys)

    def when(flag, act):
        if flag is None:
            act()
        else:
            pl.when(flag)(act)

    y_to = lax.rem(row, C) // 2
    core_to = lax.rem(z, 2)
    col_to = y_to * 2 + core_to
    off_to = mod4(y - y_to)
    index_to = jnp.where(off_to == 0, 0, jnp.where(off_to == 3, 1, jnp.where(off_to == 1, 2, 3)))
    kk_to = 2 * index_to + jnp.where(core == core_to, 0, 1)
    sx_to = 1 - 2 * (y_to // 2)
    sz_to = 1 - 2 * core_to
    counts = [len(heads) - 1 for heads, _ in PATTERNS]
    count_to = chain(kk_to, range(8), counts)
    helpers_to = []
    for n in range(max(counts)):
        having = [kk for kk in range(8) if counts[kk] > n]
        step = chain(kk_to, having, [PATTERNS[kk][0][n + 1] for kk in having])
        peer = (mod4(x + sx_to * (step // 4)) * 4 + mod4(z + sz_to * lax.rem(step, 4)), col_to)
        helpers_to.append((peer, None if len(having) == 8 else count_to > n))

    barrier = pltpu.get_barrier_semaphore()
    for peer in line_peers + plane_peers:
        pl.semaphore_signal(barrier, inc=1, device_id=peer, device_id_type=MESH)
    for kk in range(8):
        for s in range(2):
            @pl.when(helper(kk, s))
            def _():
                pl.semaphore_signal(
                    barrier, inc=1, device_id=(x0s[s] * 4 + z0, natural(kk)), device_id_type=MESH
                )

    n_h = h_sem.shape[0]
    h_rows = local_rows // n_h
    h_copies = [
        pltpu.make_async_copy(
            h_ref.at[pl.ds(i * h_rows, h_rows)], h_out.at[pl.ds(i * h_rows, h_rows)], h_sem.at[i]
        )
        for i in range(n_h)
    ]
    for copy in h_copies:
        copy.start()

    position = col * piece + lax.broadcasted_iota(jnp.int32, (piece, B), 0)
    column = lax.broadcasted_iota(jnp.int32, (piece, B), 1)
    global_block = (position >> 7) * R + row
    within = position & (B - 1)
    panel_copy.wait()
    raw = raw_panel[...]
    unit = jnp.where(column < within, raw, jnp.where(column == within, 1.0, 0.0))
    kept = jnp.where(global_block == 1, unit, 0.0)
    rows[0, col] = jnp.where(global_block >= 2, raw, kept)

    pl.semaphore_wait(barrier, len(line_peers) + len(plane_peers) + count_to)

    def remote(src, dst, send, recv, peer):
        return pltpu.make_async_remote_copy(
            src_ref=src, dst_ref=dst, send_sem=send, recv_sem=recv, device_id=peer, device_id_type=MESH
        )

    def wait_for(ref, sem):
        pltpu.make_async_copy(ref, ref, sem).wait()

    mine16 = pl.ds(pl.multiple_of(col * 16, 16), 16)

    def reduce_step(ph, step):
        if step == 0:
            for peer in line_peers:
                remote(
                    part.at[ph, pl.ds(pl.multiple_of(peer[1] * 16, 16), 16)], ar1.at[ph, col],
                    ar_send.at[ph, 0], ar_recv.at[ph, 0], peer,
                ).start()
            ar1[ph, col] = part[ph, mine16]
        elif step == 1:
            wait_for(ar1.at[ph, pl.ds(0, C - 1)], ar_recv.at[ph, 0])
            ar2[ph, row] = sum(ar1[ph, i] for i in range(C))
            for peer in plane_peers:
                remote(ar2.at[ph, row], ar2.at[ph, row], ar_send.at[ph, 1], ar_recv.at[ph, 1], peer).start()
        elif step == 2:
            wait_for(ar2.at[ph, pl.ds(0, R - 1)], ar_recv.at[ph, 1])
            arout[ph, mine16] = sum(ar2[ph, i] for i in range(R))
            for peer in line_peers:
                remote(arout.at[ph, mine16], arout.at[ph, mine16], ar_send.at[ph, 2], ar_recv.at[ph, 2], peer).start()
        else:
            wait_for(arout.at[ph, pl.ds(0, 16 * (C - 1))], ar_recv.at[ph, 2])

    def reduce_finish(ph):
        wait_for(ar1.at[ph, pl.ds(0, C - 1)], ar_send.at[ph, 0])
        wait_for(ar2.at[ph, pl.ds(0, R - 1)], ar_send.at[ph, 1])
        wait_for(ar1.at[ph, pl.ds(0, C - 1)], ar_send.at[ph, 2])

    am_root = col == col_to
    other_root = other == col_to
    OTHERS = (1, -1, 2)

    def other_is_root(off):
        return (mod4(y + off) == y_to) & (core == core_to)

    def first_sends(ph):
        here = rows.at[ph, col]
        @pl.when(jnp.logical_not(am_root))
        def _():
            remote(here, here, ysend.at[ph, 0], yrecv.at[ph, col], (row, col_to)).start()
        for peer, flag in helpers_to:
            copy = remote(here, cols.at[ph, x // 2, col], lsend.at[ph], precv.at[ph, x // 2, col], peer)
            when(flag, copy.start)

    def line_start(ph):
        here = rows.at[ph, col]
        for n, off in enumerate(OTHERS):
            @pl.when(jnp.logical_not(other_is_root(off)))
            def _():
                remote(here, here, ysend.at[ph, 1 + n], yrecv.at[ph, col], at_y(off)).start()
        @pl.when(jnp.logical_not(other_root))
        def _():
            remote(here, here, ysend.at[ph, 4], yrecv.at[ph, col], (row, other)).start()

    def line_step(ph, kk):
        k = natural(kk)
        here = rows.at[ph, k]
        @pl.when(jnp.logical_not(am_root))
        def _():
            wait_for(here, yrecv.at[ph, k])
        if kk % 2 == 0:
            @pl.when(jnp.logical_not(other_root))
            def _():
                remote(here, here, ysend.at[ph, 4 + kk // 2], yrecv.at[ph, k], (row, other)).start()

    def plane_step(ph, kk):
        k = natural(kk)
        for s in range(2):
            here = cols.at[ph, s, k]

            def send(source):
                for peer, flag in next_chips(kk, s):
                    when(flag, remote(source, here, psend.at[ph, s, kk], precv.at[ph, s, k], peer).start)

            @pl.when(roots[s])
            def _():
                if kk:
                    wait_for(rows.at[ph, k], yrecv.at[ph, k])
                send(rows.at[ph, k])

            @pl.when(helper(kk, s))
            def _():
                wait_for(here, precv.at[ph, s, k])
                send(here)

    ORDER = (0, 1, 2, 4, 3, 5, 6, 7)

    def gather(ph, extra):
        first_sends(ph)
        for tick, kk in enumerate(ORDER):
            plane_step(ph, kk)
            if tick == 4:
                line_start(ph)
            extra(tick)

    def gather_wait(ph):
        for s in range(2):
            for kk in range(8):
                k = natural(kk)
                @pl.when(jnp.logical_not(helper(kk, s) | roots[s]))
                def _():
                    wait_for(cols.at[ph, s, k], precv.at[ph, s, k])
            @pl.when(roots[s])
            def _():
                cols[ph, s] = rows[ph]

    def gather_finish(ph):
        sent = [jnp.logical_not(am_root)] + [jnp.logical_not(other_is_root(off)) for off in OTHERS]
        for n, flag in enumerate(sent + [jnp.logical_not(other_root)] * 4):
            @pl.when(flag)
            def _():
                wait_for(rows.at[ph, 0], ysend.at[ph, n])
        for count in sorted(set(counts)):
            @pl.when(count_to == count)
            def _():
                wait_for(cols.at[ph, 0, pl.ds(0, count)], lsend.at[ph])
        for kk in range(8):
            heads, groups = PATTERNS[kk]
            sizes = sorted(set(len(group) for group in groups) - {0})
            for s in range(2):
                for size in sizes:
                    keys = [head for head, group in zip(heads, groups) if len(group) == size]
                    @pl.when(among(codes[s], keys))
                    def _():
                        wait_for(cols.at[ph, 0, pl.ds(0, size)], psend.at[ph, s, kk])

    def split_h(i):
        h_copies[i].wait()
        hi, lo = halves(h_out[pl.ds(i * h_rows, h_rows)])
        hhi[pl.ds(i * h_rows, h_rows)] = hi
        hlo[pl.ds(i * h_rows, h_rows)] = lo

    def first_extra(tick):
        if tick == 0:
            part[0] = dot6(rows[0, col], rows[0, col], TN)
        if tick == 4:
            reduce_step(0, 0)
        split_h(tick)

    gather(0, first_extra)
    reduce_step(0, 1)
    gather_wait(0)

    def block_rows(ph, s, b):
        flat = cols.at[ph, s].reshape(local_rows, B)
        return flat[pl.ds(b * B, B)]

    for b in range(blocks):
        for s in range(2):
            at = pl.ds((2 * b + s) * B, B)
            hi, lo = halves(block_rows(0, s, b))
            vw[at, :B] = hi
            vw[at, B:] = lo
            zhi[at, :B] = hi
            zlo[at, :B] = lo

    order = (2, 1, -1, 0)
    two_rows = 2 * piece
    v_rows = rows.at[0].reshape(local_rows, B)
    p_rows = rows.at[1].reshape(local_rows, B)

    def part_of(j, which):
        start = mod4(y + order[j]) * two_rows + which * piece
        return pl.ds(pl.multiple_of(start, 16), piece)

    def sum_pair(j):
        wait_for(sib_in.at[j], sib_recv.at[j])
        ring_out[j] = acc[part_of(j, core)] + sib_in[j]
        if order[j]:
            remote(ring_out.at[j], ring_in.at[j], ring_send.at[j], ring_recv.at[j], at_y(order[j])).start()

    for j, off in enumerate(order):
        take = pl.ds(pl.multiple_of(mod4(y + off) * two_rows, 32), two_rows)
        both = dot1(hhi[take], vw[...]) + dot1(hlo[take], vw[...])
        acc[take] = both[:, :B] + both[:, B:]
        remote(
            acc.at[part_of(j, 1 - core)], sib_in.at[j], sib_send.at[j], sib_recv.at[j], (row, other)
        ).start()
        if j:
            sum_pair(j - 1)
    sum_pair(3)
    for kk in ORDER[1:]:
        line_step(0, kk)
    part[1] = dot6(v_rows[...], acc[...], TN)
    reduce_step(1, 0)
    reduce_step(0, 2)
    p_piece = ring_out[3]
    for j in range(3):
        wait_for(ring_in.at[j], ring_recv.at[j])
        p_piece = p_piece + ring_in[j]
    rows[1, col] = p_piece

    eye_r = lax.broadcasted_iota(jnp.int32, (B, B), 0)
    eye_c = lax.broadcasted_iota(jnp.int32, (B, B), 1)
    gram = arout.at[0]

    def inverse_step(i):
        if i == 0:
            g = gram[...]
            half = jnp.sum(jnp.where(eye_r == eye_c, g, 0.0), axis=1, keepdims=True) * 0.5
            start = -(jnp.where(eye_c > eye_r, g, 0.0) / half)
            inverse[...] = start + jnp.where(eye_r == eye_c, 1.0, 0.0)
            power[...] = dot6(start, start)
        elif i < 7:
            now = power[...]
            inverse[...] = inverse[...] + dot6(inverse[...], now)
            if i < 6:
                power[...] = dot6(now, now)
        else:
            g = gram[...]
            half = jnp.sum(jnp.where(eye_r == eye_c, g, 0.0), axis=0, keepdims=True) * 0.5
            inverse[...] = inverse[...] / half

    def second_extra(tick):
        if tick == 0:
            reduce_step(1, 1)

    gather(1, second_extra)
    reduce_step(1, 2)
    reduce_step(0, 3)
    for i in range(8):
        inverse_step(i)
    for kk in ORDER[1:]:
        line_step(1, kk)
    reduce_step(1, 3)

    u = inverse[...]
    middle = dot6(dot6(u, arout[1], TN), u)
    middle = -0.5 * (middle + middle.T)
    chunk = 384
    for t in range(local_rows // chunk):
        at = pl.ds(t * chunk, chunk)
        v, p = v_rows[at], p_rows[at]
        hi, lo = halves(dot6(p, u) + dot6(v, middle))
        whi[at, :B] = hi
        wlo[at, :B] = lo
        hi, lo = halves(dot6(v, u, NT))
        whi[at, B:] = hi
        wlo[at, B:] = lo

    gather_wait(1)
    for b in range(blocks):
        for s in range(2):
            at = pl.ds((2 * b + s) * B, B)
            hi, lo = halves(block_rows(1, s, b))
            zhi[at, B:] = hi
            zlo[at, B:] = lo

    for ph in range(2):
        gather_finish(ph)
        reduce_finish(ph)
    for j in range(4):
        wait_for(sib_in.at[j], sib_send.at[j])
    for j in range(3):
        wait_for(ring_in.at[j], ring_send.at[j])


def update_kernel(h_ref, whi, wlo, zhi, zlo, out_ref, tiles, sem):
    width = tiles.shape[2]
    slots = tiles.shape[0]
    steps = h_ref.shape[1] // width
    height = 288

    def copy(b):
        slot = lax.rem(b, slots)
        return pltpu.make_async_copy(
            tiles.at[slot], out_ref.at[:, pl.ds(pl.multiple_of(b * width, width), width)], sem.at[slot]
        )

    def step(b, carry):
        @pl.when(b >= slots)
        def _():
            copy(b - slots).wait()

        at = pl.ds(pl.multiple_of(b * width, width), width)
        high, low = zhi[at], zlo[at]
        for start in range(0, h_ref.shape[0], height):
            take = pl.ds(start, height)
            w = whi[take]
            change = dot1(w, high, NT) + dot1(wlo[take], high, NT) + dot1(w, low, NT)
            tiles[lax.rem(b, slots), take] = h_ref[take, at] - change
        copy(b).start()
        return carry

    lax.fori_loop(0, steps, step, 0)
    for b in range(steps - slots, steps):
        copy(b).wait()


def body(hamiltonian, panel):
    m, n = hamiltonian.shape
    piece = panel.shape[0]
    vmem = pl.BlockSpec(memory_space=pltpu.VMEM)
    hbm = pl.BlockSpec(memory_space=pl.ANY)
    dma = pltpu.SemaphoreType.DMA
    operands = pl.pallas_call(
        panel_kernel,
        out_shape=[
            jax.ShapeDtypeStruct((m, n), F32),
            jax.ShapeDtypeStruct((m, 2 * B), BF16),
            jax.ShapeDtypeStruct((m, 2 * B), BF16),
            jax.ShapeDtypeStruct((n, 2 * B), BF16),
            jax.ShapeDtypeStruct((n, 2 * B), BF16),
        ],
        in_specs=[hbm, hbm],
        out_specs=[vmem] * 5,
        scratch_shapes=[
            pltpu.VMEM((m, n), BF16),
            pltpu.VMEM((m, n), BF16),
            pltpu.VMEM((n, 2 * B), BF16),
            pltpu.VMEM((2, C, piece, B), F32),
            pltpu.VMEM((2, 2, C, piece, B), F32),
            pltpu.VMEM((m, B), F32),
            pltpu.VMEM((4, piece, B), F32),
            pltpu.VMEM((3, piece, B), F32),
            pltpu.VMEM((4, piece, B), F32),
            pltpu.VMEM((piece, B), F32),
            pltpu.VMEM((2, B, B), F32),
            pltpu.VMEM((2, C, 16, B), F32),
            pltpu.VMEM((2, R, 16, B), F32),
            pltpu.VMEM((2, B, B), F32),
            pltpu.VMEM((B, B), F32),
            pltpu.VMEM((B, B), F32),
            dma,
            dma((8,)),
            dma((2, 8)),
            dma((2, C)),
            dma((2,)),
            dma((2, 2, C)),
            dma((2, 2, C)),
            dma((4,)),
            dma((4,)),
            dma((3,)),
            dma((3,)),
            dma((2, 3)),
            dma((2, 3)),
        ],
        compiler_params=pltpu.CompilerParams(
            collective_id=0, has_side_effects=True, vmem_limit_bytes=40 * 2**20
        ),
        cost_estimate=pl.CostEstimate(flops=8 * m * n * B, bytes_accessed=4 * m * n, transcendentals=0),
        name="panel_products",
    )(hamiltonian, pltpu.with_memory_space_constraint(panel, pltpu.HBM))
    return pl.pallas_call(
        update_kernel,
        out_shape=jax.ShapeDtypeStruct((m, n), F32),
        in_specs=[vmem] * 5,
        out_specs=hbm,
        scratch_shapes=[pltpu.VMEM((2, m, 6 * B), F32), dma((2,))],
        compiler_params=pltpu.CompilerParams(vmem_limit_bytes=24 * 2**20),
        cost_estimate=pl.CostEstimate(flops=12 * m * n * B, bytes_accessed=4 * m * n, transcendentals=0),
        name="rank_update",
    )(*operands)


def solution(mesh):
    return jax.shard_map(
        body,
        mesh=mesh,
        in_specs=(P("row", "col"), P(("row", "col"), None)),
        out_specs=P("row", "col"),
        check_vma=False,
    )
```

```python
import jax
import jax.numpy as jnp
from jax import lax
from jax.experimental import pallas as pl
from jax.experimental.pallas import tpu as pltpu
from jax.sharding import PartitionSpec as P

B = 128
R = 16
C = 8
MESH = pl.DeviceIdType.MESH
F32 = jnp.float32
BF16 = jnp.bfloat16
HIGHEST = lax.Precision.HIGHEST

PATTERNS = (
    ((0, 2, 4, 8, 11, 12, 13), ((), (1, 3, 6, 14), (5, 7), (), (10, 15), (), (9,))),
    ((0, 1, 4, 7, 8, 11, 12, 15), ((), (2, 13), (5,), (3, 6), (9,), (10,), (), (14,))),
    ((0, 2, 4, 11, 13), ((3,), (1, 6, 14), (5,), (7, 8, 10, 15), (9, 12))),
    ((0, 5, 7, 8, 14), ((1,), (9,), (3, 4, 6, 11), (12,), (2, 10, 13, 15))),
    ((0, 2, 4, 9, 12), ((), (1, 3, 6, 14), (5, 7, 8), (10, 11, 13), (15,))),
    ((0, 5, 7, 8, 14), ((3,), (1, 9), (4, 6), (11, 12), (2, 10, 13, 15))),
    ((0, 5, 7, 14), ((8, 12), (1, 6, 9, 13), (3, 4, 11), (2, 10, 15))),
    ((0, 9, 10, 15), ((1, 4, 12), (5, 8, 13), (2, 6, 11, 14), (3, 7))),
)
NN = (((1,), (0,)), ((), ()))
NT = (((1,), (1,)), ((), ()))
TN = (((0,), (0,)), ((), ()))


def dot6(a, b, dims=NN):
    return lax.dot_general(a, b, dims, precision=HIGHEST, preferred_element_type=F32)


def dot1(a, b, dims=NN):
    return lax.dot_general(a, b, dims, preferred_element_type=F32)


def halves(v):
    hi = v.astype(BF16)
    return hi, (v - hi.astype(F32)).astype(BF16)


def mod4(v):
    return lax.rem(v + 8, 4)


def panel_kernel(
    h_ref, panel_ref, h_out, whi, wlo, zhi, zlo,
    hhi, hlo, vw, rows, cols, acc, sib_in, ring_in, ring_out, raw_panel,
    part, ar1, ar2, arout, power, inverse,
    p_sem, h_sem, ysend, yrecv, lsend, psend, precv, sib_send, sib_recv, ring_send, ring_recv, ar_send, ar_recv,
):
    row = lax.axis_index("row")
    col = lax.axis_index("col")
    x, z = row // 4, lax.rem(row, 4)
    y, core = col // 2, lax.rem(col, 2)
    other = col + 1 - 2 * core
    panel_copy = pltpu.make_async_copy(panel_ref, raw_panel, p_sem)
    panel_copy.start()
    piece = panel_ref.shape[0]
    local_rows = h_out.shape[0]
    blocks = local_rows // B

    def at_y(off):
        return (row, mod4(y + off) * 2 + core)

    line_peers = [(row, lax.rem(col + o, C)) for o in range(1, C)]
    plane_peers = [(lax.rem(row + o, R), col) for o in range(1, R)]

    sz = 1 - 2 * core
    sx = 1 - 2 * (y // 2)
    z0 = 2 * lax.rem(y, 2) + core
    x0s = [y // 2, y // 2 + 2]
    codes = [4 * mod4((x - x0) * sx) + mod4((z - z0) * sz) for x0 in x0s]
    roots = [code == 0 for code in codes]
    OFFS = (0, -1, 1, 2)

    def natural(kk):
        return mod4(y + OFFS[kk // 2]) * 2 + (core if kk % 2 == 0 else 1 - core)

    def chain(key, keys, values):
        out = values[0]
        for k, v in zip(keys[1:], values[1:]):
            out = jnp.where(key == k, v, out)
        return out

    def among(key, keys):
        found = key == keys[0]
        for k in keys[1:]:
            found = found | (key == k)
        return found

    def helper(kk, s):
        return among(codes[s], PATTERNS[kk][0][1:])

    def next_chips(kk, s):
        heads, groups = PATTERNS[kk]
        for n in range(max(len(group) for group in groups)):
            pairs = [(head, group[n]) for head, group in zip(heads, groups) if len(group) > n]
            keys = [head for head, _ in pairs]
            steps = [4 * ((to // 4 - head // 4) % 4) + (to % 4 - head % 4) % 4 for head, to in pairs]
            step = chain(codes[s], keys, steps)
            peer = (mod4(x + sx * (step // 4)) * 4 + mod4(z + sz * lax.rem(step, 4)), col)
            yield peer, None if len(keys) == len(heads) else among(codes[s], keys)

    def when(flag, act):
        if flag is None:
            act()
        else:
            pl.when(flag)(act)

    y_to = lax.rem(row, C) // 2
    core_to = lax.rem(z, 2)
    col_to = y_to * 2 + core_to
    off_to = mod4(y - y_to)
    index_to = jnp.where(off_to == 0, 0, jnp.where(off_to == 3, 1, jnp.where(off_to == 1, 2, 3)))
    kk_to = 2 * index_to + jnp.where(core == core_to, 0, 1)
    sx_to = 1 - 2 * (y_to // 2)
    sz_to = 1 - 2 * core_to
    counts = [len(heads) - 1 for heads, _ in PATTERNS]
    count_to = chain(kk_to, range(8), counts)
    helpers_to = []
    for n in range(max(counts)):
        having = [kk for kk in range(8) if counts[kk] > n]
        step = chain(kk_to, having, [PATTERNS[kk][0][n + 1] for kk in having])
        peer = (mod4(x + sx_to * (step // 4)) * 4 + mod4(z + sz_to * lax.rem(step, 4)), col_to)
        helpers_to.append((peer, None if len(having) == 8 else count_to > n))

    barrier = pltpu.get_barrier_semaphore()
    for peer in line_peers + plane_peers:
        pl.semaphore_signal(barrier, inc=1, device_id=peer, device_id_type=MESH)
    for kk in range(8):
        for s in range(2):
            @pl.when(helper(kk, s))
            def _():
                pl.semaphore_signal(
                    barrier, inc=1, device_id=(x0s[s] * 4 + z0, natural(kk)), device_id_type=MESH
                )

    n_h = h_sem.shape[0]
    h_rows = local_rows // n_h
    h_copies = [
        pltpu.make_async_copy(
            h_ref.at[pl.ds(i * h_rows, h_rows)], h_out.at[pl.ds(i * h_rows, h_rows)], h_sem.at[i]
        )
        for i in range(n_h)
    ]
    for copy in h_copies:
        copy.start()

    position = col * piece + lax.broadcasted_iota(jnp.int32, (piece, B), 0)
    column = lax.broadcasted_iota(jnp.int32, (piece, B), 1)
    global_block = (position >> 7) * R + row
    within = position & (B - 1)
    panel_copy.wait()
    raw = raw_panel[...]
    unit = jnp.where(column < within, raw, jnp.where(column == within, 1.0, 0.0))
    kept = jnp.where(global_block == 1, unit, 0.0)
    rows[0, col] = jnp.where(global_block >= 2, raw, kept)

    pl.semaphore_wait(barrier, len(line_peers) + len(plane_peers) + count_to)

    def remote(src, dst, send, recv, peer):
        return pltpu.make_async_remote_copy(
            src_ref=src, dst_ref=dst, send_sem=send, recv_sem=recv, device_id=peer, device_id_type=MESH
        )

    def wait_for(ref, sem):
        pltpu.make_async_copy(ref, ref, sem).wait()

    mine16 = pl.ds(pl.multiple_of(col * 16, 16), 16)

    def reduce_step(ph, step):
        if step == 0:
            for peer in line_peers:
                remote(
                    part.at[ph, pl.ds(pl.multiple_of(peer[1] * 16, 16), 16)], ar1.at[ph, col],
                    ar_send.at[ph, 0], ar_recv.at[ph, 0], peer,
                ).start()
            ar1[ph, col] = part[ph, mine16]
        elif step == 1:
            wait_for(ar1.at[ph, pl.ds(0, C - 1)], ar_recv.at[ph, 0])
            ar2[ph, row] = sum(ar1[ph, i] for i in range(C))
            for peer in plane_peers:
                remote(ar2.at[ph, row], ar2.at[ph, row], ar_send.at[ph, 1], ar_recv.at[ph, 1], peer).start()
        elif step == 2:
            wait_for(ar2.at[ph, pl.ds(0, R - 1)], ar_recv.at[ph, 1])
            arout[ph, mine16] = sum(ar2[ph, i] for i in range(R))
            for peer in line_peers:
                remote(arout.at[ph, mine16], arout.at[ph, mine16], ar_send.at[ph, 2], ar_recv.at[ph, 2], peer).start()
        else:
            wait_for(arout.at[ph, pl.ds(0, 16 * (C - 1))], ar_recv.at[ph, 2])

    def reduce_finish(ph):
        wait_for(ar1.at[ph, pl.ds(0, C - 1)], ar_send.at[ph, 0])
        wait_for(ar2.at[ph, pl.ds(0, R - 1)], ar_send.at[ph, 1])
        wait_for(ar1.at[ph, pl.ds(0, C - 1)], ar_send.at[ph, 2])

    am_root = col == col_to
    other_root = other == col_to
    OTHERS = (1, -1, 2)

    def other_is_root(off):
        return (mod4(y + off) == y_to) & (core == core_to)

    def first_sends(ph):
        here = rows.at[ph, col]
        @pl.when(jnp.logical_not(am_root))
        def _():
            remote(here, here, ysend.at[ph, 0], yrecv.at[ph, col], (row, col_to)).start()
        for peer, flag in helpers_to:
            copy = remote(here, cols.at[ph, x // 2, col], lsend.at[ph], precv.at[ph, x // 2, col], peer)
            when(flag, copy.start)

    def line_start(ph):
        here = rows.at[ph, col]
        for n, off in enumerate(OTHERS):
            @pl.when(jnp.logical_not(other_is_root(off)))
            def _():
                remote(here, here, ysend.at[ph, 1 + n], yrecv.at[ph, col], at_y(off)).start()
        @pl.when(jnp.logical_not(other_root))
        def _():
            remote(here, here, ysend.at[ph, 4], yrecv.at[ph, col], (row, other)).start()

    def line_step(ph, kk):
        k = natural(kk)
        here = rows.at[ph, k]
        @pl.when(jnp.logical_not(am_root))
        def _():
            wait_for(here, yrecv.at[ph, k])
        if kk % 2 == 0:
            @pl.when(jnp.logical_not(other_root))
            def _():
                remote(here, here, ysend.at[ph, 4 + kk // 2], yrecv.at[ph, k], (row, other)).start()

    def plane_step(ph, kk):
        k = natural(kk)
        for s in range(2):
            here = cols.at[ph, s, k]

            def send(source):
                for peer, flag in next_chips(kk, s):
                    when(flag, remote(source, here, psend.at[ph, s, kk], precv.at[ph, s, k], peer).start)

            @pl.when(roots[s])
            def _():
                if kk:
                    wait_for(rows.at[ph, k], yrecv.at[ph, k])
                send(rows.at[ph, k])

            @pl.when(helper(kk, s))
            def _():
                wait_for(here, precv.at[ph, s, k])
                send(here)

    ORDER = (0, 1, 2, 4, 3, 5, 6, 7)

    def gather(ph, extra):
        first_sends(ph)
        for tick, kk in enumerate(ORDER):
            plane_step(ph, kk)
            if tick == 4:
                line_start(ph)
            extra(tick)

    def gather_wait(ph):
        for s in range(2):
            for kk in range(8):
                k = natural(kk)
                @pl.when(jnp.logical_not(helper(kk, s) | roots[s]))
                def _():
                    wait_for(cols.at[ph, s, k], precv.at[ph, s, k])
            @pl.when(roots[s])
            def _():
                cols[ph, s] = rows[ph]

    def gather_finish(ph):
        sent = [jnp.logical_not(am_root)] + [jnp.logical_not(other_is_root(off)) for off in OTHERS]
        for n, flag in enumerate(sent + [jnp.logical_not(other_root)] * 4):
            @pl.when(flag)
            def _():
                wait_for(rows.at[ph, 0], ysend.at[ph, n])
        for count in sorted(set(counts)):
            @pl.when(count_to == count)
            def _():
                wait_for(cols.at[ph, 0, pl.ds(0, count)], lsend.at[ph])
        for kk in range(8):
            heads, groups = PATTERNS[kk]
            sizes = sorted(set(len(group) for group in groups) - {0})
            for s in range(2):
                for size in sizes:
                    keys = [head for head, group in zip(heads, groups) if len(group) == size]
                    @pl.when(among(codes[s], keys))
                    def _():
                        wait_for(cols.at[ph, 0, pl.ds(0, size)], psend.at[ph, s, kk])

    def split_h(i):
        h_copies[i].wait()
        hi, lo = halves(h_out[pl.ds(i * h_rows, h_rows)])
        hhi[pl.ds(i * h_rows, h_rows)] = hi
        hlo[pl.ds(i * h_rows, h_rows)] = lo

    def first_extra(tick):
        if tick == 0:
            part[0] = dot6(rows[0, col], rows[0, col], TN)
        if tick == 4:
            reduce_step(0, 0)
        split_h(tick)

    gather(0, first_extra)
    reduce_step(0, 1)
    gather_wait(0)

    def block_rows(ph, s, b):
        flat = cols.at[ph, s].reshape(local_rows, B)
        return flat[pl.ds(b * B, B)]

    for b in range(blocks):
        for s in range(2):
            at = pl.ds((2 * b + s) * B, B)
            hi, lo = halves(block_rows(0, s, b))
            vw[at, :B] = hi
            vw[at, B:] = lo

    order = (2, 1, -1, 0)
    two_rows = 2 * piece
    v_rows = rows.at[0].reshape(local_rows, B)
    p_rows = rows.at[1].reshape(local_rows, B)

    def part_of(j, which):
        start = mod4(y + order[j]) * two_rows + which * piece
        return pl.ds(pl.multiple_of(start, 16), piece)

    def sum_pair(j):
        wait_for(sib_in.at[j], sib_recv.at[j])
        ring_out[j] = acc[part_of(j, core)] + sib_in[j]
        if order[j]:
            remote(ring_out.at[j], ring_in.at[j], ring_send.at[j], ring_recv.at[j], at_y(order[j])).start()

    for j, off in enumerate(order):
        take = pl.ds(pl.multiple_of(mod4(y + off) * two_rows, 32), two_rows)
        both = dot1(hhi[take], vw[...]) + dot1(hlo[take], vw[...])
        acc[take] = both[:, :B] + both[:, B:]
        remote(
            acc.at[part_of(j, 1 - core)], sib_in.at[j], sib_send.at[j], sib_recv.at[j], (row, other)
        ).start()
        if j:
            sum_pair(j - 1)
    sum_pair(3)
    for kk in ORDER[1:]:
        line_step(0, kk)
    part[1] = dot6(v_rows[...], acc[...], TN)
    reduce_step(1, 0)
    reduce_step(0, 2)
    p_piece = ring_out[3]
    for j in range(3):
        wait_for(ring_in.at[j], ring_recv.at[j])
        p_piece = p_piece + ring_in[j]
    rows[1, col] = p_piece

    eye_r = lax.broadcasted_iota(jnp.int32, (B, B), 0)
    eye_c = lax.broadcasted_iota(jnp.int32, (B, B), 1)
    gram = arout.at[0]

    def inverse_step(i):
        if i == 0:
            g = gram[...]
            half = jnp.sum(jnp.where(eye_r == eye_c, g, 0.0), axis=1, keepdims=True) * 0.5
            start = -(jnp.where(eye_c > eye_r, g, 0.0) / half)
            inverse[...] = start + jnp.where(eye_r == eye_c, 1.0, 0.0)
            power[...] = dot6(start, start)
        elif i < 7:
            now = power[...]
            inverse[...] = inverse[...] + dot6(inverse[...], now)
            if i < 6:
                power[...] = dot6(now, now)
        else:
            g = gram[...]
            half = jnp.sum(jnp.where(eye_r == eye_c, g, 0.0), axis=0, keepdims=True) * 0.5
            inverse[...] = inverse[...] / half

    def second_extra(tick):
        if tick == 0:
            reduce_step(1, 1)

    gather(1, second_extra)
    reduce_step(1, 2)
    reduce_step(0, 3)
    for i in range(8):
        inverse_step(i)
    for kk in ORDER[1:]:
        line_step(1, kk)
    reduce_step(1, 3)

    u = inverse[...]
    middle = dot6(dot6(u, arout[1], TN), u)
    middle = -0.5 * (middle + middle.T)
    chunk = 384
    for t in range(local_rows // chunk):
        at = pl.ds(t * chunk, chunk)
        v, p = v_rows[at], p_rows[at]
        hi, lo = halves(dot6(p, u) + dot6(v, middle))
        whi[at, :B] = hi
        wlo[at, :B] = lo
        hi, lo = halves(dot6(v, u, NT))
        whi[at, B:] = hi
        wlo[at, B:] = lo

    zhi[:, :B] = vw[:, :B]
    zlo[:, :B] = vw[:, B:]
    gather_wait(1)
    for b in range(blocks):
        for s in range(2):
            at = pl.ds((2 * b + s) * B, B)
            hi, lo = halves(block_rows(1, s, b))
            zhi[at, B:] = hi
            zlo[at, B:] = lo

    for ph in range(2):
        gather_finish(ph)
        reduce_finish(ph)
    for j in range(4):
        wait_for(sib_in.at[j], sib_send.at[j])
    for j in range(3):
        wait_for(ring_in.at[j], ring_send.at[j])


def update_kernel(h_ref, whi, wlo, zhi, zlo, out_ref, tiles, sem):
    width = tiles.shape[2]
    slots = tiles.shape[0]
    steps = h_ref.shape[1] // width
    height = 288

    def copy(b):
        slot = lax.rem(b, slots)
        return pltpu.make_async_copy(
            tiles.at[slot], out_ref.at[:, pl.ds(pl.multiple_of(b * width, width), width)], sem.at[slot]
        )

    def step(b, carry):
        @pl.when(b >= slots)
        def _():
            copy(b - slots).wait()

        at = pl.ds(pl.multiple_of(b * width, width), width)
        high, low = zhi[at], zlo[at]
        for start in range(0, h_ref.shape[0], height):
            take = pl.ds(start, height)
            w = whi[take]
            change = dot1(w, high, NT) + dot1(wlo[take], high, NT) + dot1(w, low, NT)
            tiles[lax.rem(b, slots), take] = h_ref[take, at] - change
        copy(b).start()
        return carry

    lax.fori_loop(0, steps, step, 0)
    for b in range(steps - slots, steps):
        copy(b).wait()


def body(hamiltonian, panel):
    m, n = hamiltonian.shape
    piece = panel.shape[0]
    vmem = pl.BlockSpec(memory_space=pltpu.VMEM)
    hbm = pl.BlockSpec(memory_space=pl.ANY)
    dma = pltpu.SemaphoreType.DMA
    operands = pl.pallas_call(
        panel_kernel,
        out_shape=[
            jax.ShapeDtypeStruct((m, n), F32),
            jax.ShapeDtypeStruct((m, 2 * B), BF16),
            jax.ShapeDtypeStruct((m, 2 * B), BF16),
            jax.ShapeDtypeStruct((n, 2 * B), BF16),
            jax.ShapeDtypeStruct((n, 2 * B), BF16),
        ],
        in_specs=[hbm, hbm],
        out_specs=[vmem] * 5,
        scratch_shapes=[
            pltpu.VMEM((m, n), BF16),
            pltpu.VMEM((m, n), BF16),
            pltpu.VMEM((n, 2 * B), BF16),
            pltpu.VMEM((2, C, piece, B), F32),
            pltpu.VMEM((2, 2, C, piece, B), F32),
            pltpu.VMEM((m, B), F32),
            pltpu.VMEM((4, piece, B), F32),
            pltpu.VMEM((3, piece, B), F32),
            pltpu.VMEM((4, piece, B), F32),
            pltpu.VMEM((piece, B), F32),
            pltpu.VMEM((2, B, B), F32),
            pltpu.VMEM((2, C, 16, B), F32),
            pltpu.VMEM((2, R, 16, B), F32),
            pltpu.VMEM((2, B, B), F32),
            pltpu.VMEM((B, B), F32),
            pltpu.VMEM((B, B), F32),
            dma,
            dma((8,)),
            dma((2, 8)),
            dma((2, C)),
            dma((2,)),
            dma((2, 2, C)),
            dma((2, 2, C)),
            dma((4,)),
            dma((4,)),
            dma((3,)),
            dma((3,)),
            dma((2, 3)),
            dma((2, 3)),
        ],
        compiler_params=pltpu.CompilerParams(
            collective_id=0, has_side_effects=True, vmem_limit_bytes=40 * 2**20
        ),
        cost_estimate=pl.CostEstimate(flops=8 * m * n * B, bytes_accessed=4 * m * n, transcendentals=0),
        name="panel_products",
    )(hamiltonian, pltpu.with_memory_space_constraint(panel, pltpu.HBM))
    return pl.pallas_call(
        update_kernel,
        out_shape=jax.ShapeDtypeStruct((m, n), F32),
        in_specs=[vmem] * 5,
        out_specs=hbm,
        scratch_shapes=[pltpu.VMEM((2, m, 6 * B), F32), dma((2,))],
        compiler_params=pltpu.CompilerParams(vmem_limit_bytes=24 * 2**20),
        cost_estimate=pl.CostEstimate(flops=12 * m * n * B, bytes_accessed=4 * m * n, transcendentals=0),
        name="rank_update",
    )(*operands)


def solution(mesh):
    return jax.shard_map(
        body,
        mesh=mesh,
        in_specs=(P("row", "col"), P(("row", "col"), None)),
        out_specs=P("row", "col"),
        check_vma=False,
    )
```
